256 devices in a mesh: src: 32 (over x, z), tgt: 8 (over y, core).
Axes of the slice: x: 4, y: 4, z: 8, core: 2. Of those that a mesh axis runs over, the one named last changes fastest.
Arguments:
- src_points: float32 [64, 16384], P(None, 'src'), may hold values from -0.43 to 0.43
- tgt_points: float32 [64, 32768], P(None, 'tgt'), may hold values from -0.43 to 0.43
- src_potential: float32 [16384], P('src'), may hold values from -1 to 1
- tgt_potential: float32 [32768], P('tgt'), may hold values from -1 to 1
- src_rhs: float32 [16384], P('src'), may hold values from -16 to 16
- tgt_rhs: float32 [32768], P('tgt'), may hold values from -16 to 16
Outputs:
- sol_src: float32 [16384], P('src')
- sol_tgt: float32 [32768], P('tgt')
- grad_src: float32 [64, 16384], P(None, 'src')
- grad_tgt: float32 [64, 32768], P(None, 'tgt')
The draws below stay inside these ranges and needn't reach their ends.
All inputs are finite; a program needn't handle non-finite values.
Results may differ from the reference program's by a relative error of at most 0.0001.
Values sent between devices are 32-bit elements; how exact they have to be, the bound alone decides.
A program may use at most 64 MiB of HBM per device.

```python
import math
import jax
import jax.numpy as jnp
from jax import lax

DIM = 64
ITERS = 3
SOURCES = 16384
TARGETS = 32768


def group_labels(key, salt, length):
    return jax.random.randint(jax.random.fold_in(key, salt), (length,), 0, 4).astype(jnp.int32)


def group_centres(key):
    signs = jax.random.randint(jax.random.fold_in(key, 5), (DIM, 4), 0, 2)
    return (2 * signs - 1).astype(jnp.float32)


def placed_points(centres, labels, key, length):
    spread = jax.random.uniform(key, (DIM, length), jnp.float32, -0.3, 0.3)
    return 0.13 * centres[:, labels] + spread


def rising_draw(key, length):
    position = jnp.arange(length).astype(jnp.float32) / length
    values = jnp.clip(jax.random.normal(key, (length,), jnp.float32), -4.0, 4.0)
    return values * (1.0 + 2.0 * position)


def group_levels(key):
    return jax.random.permutation(key, jnp.array([-2.0, -0.7, 0.7, 2.0], jnp.float32))


def draw_src_points(key, part):
    centres = group_centres(key)
    labels = group_labels(key, 101, SOURCES)
    key = jax.random.fold_in(key, 31)
    return placed_points(centres, labels, key, SOURCES)


def draw_tgt_points(key, part):
    centres = group_centres(key)
    labels = group_labels(key, 202, TARGETS)
    key = jax.random.fold_in(key, 37)
    return placed_points(centres, labels, key, TARGETS)


def draw_src_rhs(key, part):
    labels = group_labels(key, 101, SOURCES)
    key = jax.random.fold_in(key, 11)
    levels = group_levels(jax.random.fold_in(key, 3))
    return rising_draw(jax.random.fold_in(key, 4), SOURCES) + levels[labels]


def draw_tgt_rhs(key, part):
    labels = group_labels(key, 202, TARGETS)
    key = jax.random.fold_in(key, 23)
    levels = group_levels(jax.random.fold_in(key, 3))
    return rising_draw(jax.random.fold_in(key, 4), TARGETS) + levels[labels]


def shard_levels(stream_key, dims, split, smallest, largest):
    loudness = 1.0
    for dim, blocks in split:
        heights = jax.random.uniform(jax.random.fold_in(jax.random.fold_in(stream_key, 6), dim), (blocks,), jnp.float32, smallest / len(split), largest / len(split))
        loudness = loudness * jnp.repeat(jnp.exp(heights), dims[dim] // blocks).reshape((-1,) + (1,) * (len(dims) - 1 - dim))
    return loudness


def setup_inputs(seed: int = 0) -> dict:
    key_of = jax.random.split(jax.random.key(seed), 7)
    return {
        "src_points": draw_src_points(jax.random.fold_in(key_of[6], 71), 0),
        "tgt_points": draw_tgt_points(jax.random.fold_in(key_of[6], 71), 0),
        "src_potential": jnp.clip(jax.random.uniform(key_of[2], (SOURCES,), jnp.float32, -1.0, 1.0) * shard_levels(key_of[2], (SOURCES,), ((0, 32),), -0.4, 0.0), -1.0, 1.0),
        "tgt_potential": jnp.clip(jax.random.uniform(key_of[3], (TARGETS,), jnp.float32, -1.0, 1.0) * shard_levels(key_of[3], (TARGETS,), ((0, 8),), -0.4, 0.0), -1.0, 1.0),
        "src_rhs": draw_src_rhs(jax.random.fold_in(key_of[6], 71), 0),
        "tgt_rhs": draw_tgt_rhs(jax.random.fold_in(key_of[6], 71), 0),
    }


EPSILON = 0.5
REGULARIZER = 1.0
HIGHEST = lax.Precision.HIGHEST

def reference(src_points, tgt_points, src_potential, tgt_potential, src_rhs, tgt_rhs):
    normalizer = 1.0 / math.sqrt(SOURCES * TARGETS)
    block_rows = math.gcd(SOURCES, 512)
    blocks = SOURCES // block_rows
    blocked_x = src_points.reshape(DIM, blocks, block_rows).transpose(1, 0, 2)
    blocked_f = src_potential.reshape(blocks, block_rows)

    def plan_rows(x_block, f_block):
        cross_term = jnp.dot(x_block.T, tgt_points, precision=HIGHEST, preferred_element_type=jnp.float32)
        return jnp.exp(cross_term / EPSILON + f_block[:, None] + tgt_potential[None, :]) * normalizer

    def products(vec_src, vec_tgt):
        blocked_s = vec_src.reshape(blocks, block_rows)

        def scan_step(col_sum, pieces):
            x_block, f_block, s_block = pieces
            plan_block = plan_rows(x_block, f_block)
            row_out = jnp.dot(plan_block, vec_tgt, precision=HIGHEST)
            return (col_sum + jnp.dot(s_block, plan_block, precision=HIGHEST), row_out)
        col_sum, row_out = lax.scan(scan_step, jnp.zeros((TARGETS,), jnp.float32), (blocked_x, blocked_f, blocked_s))
        return (row_out.reshape(SOURCES), col_sum)
    mass_src, mass_tgt = products(jnp.ones((SOURCES,), jnp.float32), jnp.ones((TARGETS,), jnp.float32))

    def operator(vec_src, vec_tgt):
        row_out, col_out = products(vec_src, vec_tgt)
        return ((mass_src + REGULARIZER) * vec_src + row_out, (mass_tgt + REGULARIZER) * vec_tgt + col_out)

    def inner_product(a_src, a_tgt, b_src, b_tgt):
        return jnp.sum(a_src * b_src) + jnp.sum(a_tgt * b_tgt)
    sol_src = jnp.zeros((SOURCES,), jnp.float32)
    sol_tgt = jnp.zeros((TARGETS,), jnp.float32)
    res_src, res_tgt = (src_rhs, tgt_rhs)
    dir_src, dir_tgt = (src_rhs, tgt_rhs)
    norm_now = inner_product(res_src, res_tgt, res_src, res_tgt)
    for repeat in range(ITERS):
        img_src, img_tgt = operator(dir_src, dir_tgt)
        step_size = norm_now / inner_product(dir_src, dir_tgt, img_src, img_tgt)
        sol_src = sol_src + step_size * dir_src
        sol_tgt = sol_tgt + step_size * dir_tgt
        res_src = res_src - step_size * img_src
        res_tgt = res_tgt - step_size * img_tgt
        norm_next = inner_product(res_src, res_tgt, res_src, res_tgt)
        direction_ratio = norm_next / norm_now
        dir_src = res_src + direction_ratio * dir_src
        dir_tgt = res_tgt + direction_ratio * dir_tgt
        norm_now = norm_next
    blocked_u = sol_src.reshape(blocks, block_rows)

    def grad_step(carry, pieces):
        x_block, f_block, u_block = pieces
        weight = plan_rows(x_block, f_block) * (1.0 + u_block[:, None] + sol_tgt[None, :])
        row_weight = lax.optimization_barrier(jnp.sum(weight, axis=1))
        weighted_y = lax.dot_general(tgt_points, weight, (((1,), (1,)), ((), ())), precision=HIGHEST)
        col_weight = carry[0] + lax.optimization_barrier(jnp.sum(weight, axis=0))
        weighted_x = carry[1] + jnp.dot(x_block, weight, precision=HIGHEST)
        return ((col_weight, weighted_x), (row_weight, weighted_y))
    start = (jnp.zeros((TARGETS,), jnp.float32), jnp.zeros((DIM, TARGETS), jnp.float32))
    (col_weight, weighted_x), (row_weight, weighted_y) = lax.scan(grad_step, start, (blocked_x, blocked_f, blocked_u))
    row_weight = row_weight.reshape(SOURCES)
    weighted_y = weighted_y.transpose(1, 0, 2).reshape(DIM, SOURCES)
    grad_src = (row_weight[None, :] * src_points - weighted_y) / EPSILON
    grad_tgt = (col_weight[None, :] * tgt_points - weighted_x) / EPSILON
    return (sol_src, sol_tgt, grad_src, grad_tgt)
```

```python
import functools
import math

import jax
import jax.numpy as jnp
from jax import lax
from jax.experimental import pallas as pl
from jax.experimental.pallas import tpu as pltpu
from jax.sharding import PartitionSpec as P

EPSILON = 0.5
REGULARIZER = 1.0
LOG2E = math.log2(math.e)
MESH = pl.DeviceIdType.MESH
F32 = jnp.float32
BF16 = jnp.bfloat16

XS, ZS = 4, 8
SW, TW = XS * ZS, 8
DIM = 64
NS, NT = 512, 4096
SUB = NT // SW
TILE = 512
STACK = 80
VECS = 4

(A_COL, A_ROW, A_INIT, A_AGC, A_AGZ, A_AGS, B_COL, B_ROW, B_AGC, B_AGZ, B_AGS, C_SRC, C_TGT,
 D_ROW, D_COL, O_ROW, O_COL, G_NEAR, G_FAR, G_SIB1, G_SIB2) = range(21)
N_SEMS = 24
O_X = 20 + 4


def halves(value):
    high = value.astype(BF16)
    return high, (value - high.astype(F32)).astype(BF16)


def across(vector):
    return jnp.broadcast_to(vector, (128, vector.shape[1])).T


def along(block):
    return jnp.sum(block.T, axis=0, keepdims=True)


def tiled(block, times):
    return jnp.concatenate([block] * times, axis=1)


def total(value):
    return jnp.sum(jnp.sum(value, axis=1, keepdims=True), axis=0, keepdims=True)


def lanes(*values):
    spot = lax.broadcasted_iota(jnp.int32, (1, 128), 1)
    row = jnp.zeros((1, 128), F32)
    for index, value in enumerate(values):
        row = row + jnp.where(spot == index, value, 0.0)
    return row


def lane(row, index):
    spot = lax.broadcasted_iota(jnp.int32, (1, 128), 1)
    return jnp.sum(jnp.where(spot == index, row, 0.0), axis=1, keepdims=True)


def kernel(
    shift, xs_ref, yt_ref, f_ref, g_ref, a0_ref, b0_ref,
    sol_src_ref, sol_tgt_ref, gs_ref, gt_ref,
    plan, plan_hi, plan_lo, q_hi, q_lo, x4t, y4, zbuf, fcol, acol, racc, racc2,
    col_a, col_a_in, row_a, row_a_in, init_out, init_in, agc_a, agz_a, ags_a, ags_a_in,
    col_b, col_b_in, row_b, row_b_in, agc_b, agz_b, ags_b_in,
    sc_out, sc_in, sc2_out, sc2_in, ysub, vec_t, vec_s, stack, tsum,
    g_row, g_row_in, g_col, g_col_in, xg, send, recv,
):
    s = lax.axis_index("src")
    t = lax.axis_index("tgt")
    x, z = s // ZS, s % ZS
    core = t % 2
    sibling = (s, t + 1 - 2 * core)

    def src_peer(p):
        return (lax.rem(s + p, SW), t)

    def tgt_peer(p):
        return (s, lax.rem(t + p, TW))

    def z_peer(p):
        return (x * ZS + lax.rem(z + p, ZS), t)

    def x_peer(p):
        return (lax.rem(x + p, XS) * ZS + z, t)

    def push(src, dst, k, device, k_recv=None):
        pltpu.make_async_remote_copy(
            src_ref=src, dst_ref=dst, send_sem=send.at[k],
            recv_sem=recv.at[k if k_recv is None else k_recv],
            device_id=device, device_id_type=MESH,
        ).start()

    def push_all(ways, peer, src, dst, k):
        def step(p, carry):
            push(src(p), dst, k, peer(p))
            return carry
        lax.fori_loop(1, ways, step, 0)

    def wait_in(ref, k):
        pltpu.make_async_copy(ref, ref, recv.at[k]).wait()

    def wait_out(ref, k):
        pltpu.make_async_copy(ref, ref, send.at[k]).wait()

    def sub_of(p):
        return pl.ds(pl.multiple_of(lax.rem(s + p, SW) * SUB, SUB), SUB)

    my_sub = pl.ds(pl.multiple_of(s * SUB, SUB), SUB)
    my_tile = pl.ds(pl.multiple_of(z * TILE, TILE), TILE)

    barrier = pltpu.get_barrier_semaphore()

    def greet(ways, peer):
        def step(p, carry):
            pl.semaphore_signal(barrier, inc=1, device_id=peer(p), device_id_type=MESH)
            return carry
        lax.fori_loop(1, ways, step, 0)

    greet(SW, src_peer)
    greet(TW, tgt_peer)

    xs = jnp.concatenate([xs_ref[0], xs_ref[1]], axis=0)
    a0 = a0_ref[...]
    b0 = b0_ref[...]

    def x_parts(points):
        scaled = points * (LOG2E / EPSILON)
        high = scaled.astype(BF16).astype(F32)
        low = scaled - high
        return jnp.concatenate([high, high, low, low], axis=0).T.astype(BF16)

    x4t[...] = x_parts(xs)

    def y_step(n, carry):
        cs = pl.ds(pl.multiple_of(n * TILE, TILE), TILE)
        high, low = halves(yt_ref[:, cs])
        y4[0:64, cs] = high
        y4[64:128, cs] = low
        y4[128:192, cs] = high
        y4[192:256, cs] = low
        return carry
    lax.fori_loop(0, NT // TILE, y_step, 0)

    fcol[...] = across(f_ref[...] * LOG2E + shift)
    acol[...] = across(a0)
    racc[...] = jnp.zeros_like(racc)
    racc2[...] = jnp.zeros_like(racc2)

    def plan_step(n, carry):
        cs = pl.ds(pl.multiple_of(n * TILE, TILE), TILE)
        zbuf[...] = jnp.dot(x4t[...], y4[:, cs], preferred_element_type=F32)
        g_now = g_ref[:, cs] * LOG2E
        b_now = b0_ref[:, cs]

        def rows_step(r, sums):
            rows = pl.ds(pl.multiple_of(r * 64, 64), 64)
            p = jnp.exp2(zbuf[rows, :] + tiled(fcol[rows, :], 4) + g_now)
            plan[rows, cs] = p
            high, low = halves(p)
            plan_hi[rows, cs] = high
            plan_lo[rows, cs] = low
            racc[rows, :] += (p[:, 0:128] + p[:, 128:256]) + (p[:, 256:384] + p[:, 384:512])
            pb = p * b_now
            racc2[rows, :] += (pb[:, 0:128] + pb[:, 128:256]) + (pb[:, 256:384] + pb[:, 384:512])
            pa = p * tiled(acol[rows, :], 4)
            return (sums[0] + jnp.sum(p.reshape(8, 8, TILE), axis=0),
                    sums[1] + jnp.sum(pa.reshape(8, 8, TILE), axis=0))

        zero = jnp.zeros((8, TILE), F32)
        mass_sum, a_sum = lax.fori_loop(0, NS // 64, rows_step, (zero, zero))
        col_a[0:1, cs] = jnp.sum(mass_sum, axis=0, keepdims=True)
        col_a[1:2, cs] = jnp.sum(a_sum, axis=0, keepdims=True)
        return carry
    lax.fori_loop(0, NT // TILE, plan_step, 0)

    mass_part = along(racc[...])
    v_part = along(racc2[...])
    row_a[0:1, :] = mass_part
    row_a[1:2, :] = v_part
    init_out[0:1, :] = f_ref[...]
    init_out[1:2, :] = a0
    norm_part = total(a0 * a0) * (1.0 / TW) + total(b0 * b0) * (1.0 / SW)
    quad_part = (
        norm_part * REGULARIZER
        + total(a0 * a0 * mass_part) + total(b0 * b0 * col_a[0:1, :]) + 2.0 * total(a0 * v_part)
    )
    col_a[2:3, :] = tiled(lanes(norm_part, quad_part), SW)
    col_a[3:4, :] = jnp.zeros((1, NT), F32)

    pl.semaphore_wait(barrier, SW - 1 + TW - 1)

    push_all(SW, src_peer, lambda p: col_a.at[:, sub_of(p)], col_a_in.at[s], A_COL)
    push_all(TW, tgt_peer, lambda p: row_a, row_a_in.at[t], A_ROW)
    push_all(ZS, z_peer, lambda p: init_out, init_in.at[z], A_INIT)
    for p in (1, ZS - 1, 2, ZS - 2):
        push(xs_ref.at[core], xg.at[z, core], G_NEAR, z_peer(p))
    col_a_in[s] = col_a[:, my_sub]
    row_a_in[t] = row_a[...]
    init_in[z] = init_out[...]
    xg[z, 0] = xs_ref[0]
    xg[z, 1] = xs_ref[1]
    ysub[...] = yt_ref[:, my_tile]

    g_sub = g_ref[:, my_tile] * LOG2E

    def q_block(p, carry):
        zz = lax.rem(z + p, ZS)
        points = jnp.concatenate([xg[zz, 0], xg[zz, 1]], axis=0)
        fcol[...] = across(init_in[zz][0:1, :] * LOG2E + shift)
        zbuf[...] = jnp.dot(x_parts(points), y4[:, my_tile], preferred_element_type=F32)

        def rows_step(r, c):
            rows = pl.ds(pl.multiple_of(r * 64, 64), 64)
            value = jnp.exp2(zbuf[rows, :] + tiled(fcol[rows, :], 4) + g_sub)
            high, low = halves(value)
            q_hi[zz, rows, :] = high
            q_lo[zz, rows, :] = low
            return c
        lax.fori_loop(0, NS // 64, rows_step, 0)
        return carry

    wait_in(row_a_in.at[pl.ds(0, TW - 1)], A_ROW)
    row_full = jnp.sum(row_a_in[...], axis=0)
    agz_own = row_full
    wait_in(col_a_in.at[pl.ds(0, SW - 1)], A_COL)
    col_full = jnp.sum(col_a_in[...], axis=0)
    agc_a[:, my_sub] = col_full[0:2, :]
    ags_a[...] = col_full[2:3, :]
    agz_a[z] = agz_own

    push_all(SW, src_peer, lambda p: agc_a.at[:, my_sub], agc_a.at[:, my_sub], A_AGC)
    push_all(TW, tgt_peer, lambda p: ags_a, ags_a_in.at[t], A_AGS)
    push_all(ZS, z_peer, lambda p: agz_a.at[z], agz_a.at[z], A_AGZ)
    ags_a_in[t] = ags_a[...]
    wait_in(init_in.at[pl.ds(0, ZS - 1)], A_INIT)
    wait_in(xg.at[pl.ds(0, 4), 0], G_NEAR)
    for p in (1, ZS - 1, 2, ZS - 2):
        zz = lax.rem(z + p, ZS)
        push(xg.at[zz, core], xg.at[zz, core], G_SIB1, sibling)
    for p in (3, ZS - 3, 4):
        push(xs_ref.at[core], xg.at[z, core], G_FAR, z_peer(p))
    q_block(0, 0)

    wait_in(agz_a.at[pl.ds(0, ZS - 1)], A_AGZ)
    wait_in(ags_a_in.at[pl.ds(0, TW - 1)], A_AGS)
    wait_in(agc_a.at[:, pl.ds(0, (SW - 1) * SUB)], A_AGC)
    sums = jnp.sum(ags_a_in[...], axis=0)
    norm0 = lane(sums, 0)
    alpha0 = norm0 / lane(sums, 1)

    diag = [row_full[0:1, :] + REGULARIZER, agz_a[:, 0, :] + REGULARIZER, agc_a[0:1, :] + REGULARIZER]
    res0 = [a0, init_in[:, 1, :], b0]
    prod0 = [row_full[1:2, :], agz_a[:, 1, :], agc_a[1:2, :]]
    image0 = [d * r + v for d, r, v in zip(diag, res0, prod0)]
    res1 = [r - alpha0 * i for r, i in zip(res0, image0)]

    def matvec(vec_src, vec_tgt, columns):
        acol[...] = across(vec_src)
        half = NT // 2
        for h, acc in ((0, racc), (1, racc2)):
            spread = jnp.broadcast_to(vec_tgt[:, h * half:(h + 1) * half], (8, half))

            def step(r, sums):
                rows = pl.ds(pl.multiple_of(r * 8, 8), 8)
                p = plan[rows, h * half:(h + 1) * half]
                terms = p * spread
                parts = [terms[:, k * 128:(k + 1) * 128] for k in range(half // 128)]
                while len(parts) > 1:
                    parts = [parts[k] + parts[k + 1] for k in range(0, len(parts), 2)]
                acc[rows, :] = parts[0]
                if columns:
                    sums = sums + p * tiled(acol[rows, :], half // 128)
                return sums
            sums = lax.fori_loop(0, NS // 8, step, jnp.zeros((8, half), F32), unroll=2)
            if columns:
                col_b[0:1, h * half:(h + 1) * half] = jnp.sum(sums, axis=0, keepdims=True)
        return along(racc[...] + racc2[...])

    def scalars(res, row_part):
        norm = total(res[0] * res[0]) * (1.0 / TW) + total(res[2] * res[2]) * (1.0 / SW)
        quad = (
            total(res[0] * res[0] * diag[0]) * (1.0 / TW)
            + total(res[2] * res[2] * diag[2]) * (1.0 / SW)
            + 2.0 * total(res[0] * row_part)
        )
        return lanes(norm, quad)

    row_part = matvec(res1[0], res1[2], True)
    row_b[...] = row_part
    col_b[1:2, :] = tiled(scalars(res1, row_part), SW)

    push_all(SW, src_peer, lambda p: col_b.at[:, sub_of(p)], col_b_in.at[s], B_COL)
    push_all(TW, tgt_peer, lambda p: row_b, row_b_in.at[t], B_ROW)
    col_b_in[s] = col_b[:, my_sub]
    row_b_in[t] = row_b[...]
    wait_in(xg.at[pl.ds(0, 3), 0], G_FAR)
    for p in (3, ZS - 3, 4):
        zz = lax.rem(z + p, ZS)
        push(xg.at[zz, core], xg.at[zz, core], G_SIB2, sibling)
    wait_in(xg.at[pl.ds(0, 4), 0], G_SIB1)
    lax.fori_loop(1, 3, q_block, 0)
    lax.fori_loop(6, 8, q_block, 0)

    wait_in(row_b_in.at[pl.ds(0, TW - 1)], B_ROW)
    row_full1 = jnp.sum(row_b_in[...], axis=0)
    agz_b[z] = row_full1
    wait_in(col_b_in.at[pl.ds(0, SW - 1)], B_COL)
    col_full1 = jnp.sum(col_b_in[...], axis=0)
    agc_b[:, my_sub] = col_full1[0:1, :]
    sc2_out[0] = col_full1[1:2, :]

    push_all(SW, src_peer, lambda p: agc_b.at[:, my_sub], agc_b.at[:, my_sub], B_AGC)
    push_all(TW, tgt_peer, lambda p: sc2_out.at[0], ags_b_in.at[t], B_AGS)
    push_all(ZS, z_peer, lambda p: agz_b.at[z], agz_b.at[z], B_AGZ)
    ags_b_in[t] = sc2_out[0]
    wait_in(xg.at[pl.ds(0, 3), 0], G_SIB2)
    lax.fori_loop(3, 6, q_block, 0)

    wait_in(agz_b.at[pl.ds(0, ZS - 1)], B_AGZ)
    wait_in(ags_b_in.at[pl.ds(0, TW - 1)], B_AGS)
    wait_in(agc_b.at[:, pl.ds(0, (SW - 1) * SUB)], B_AGC)
    sums = jnp.sum(ags_b_in[...], axis=0)
    norm1 = lane(sums, 0)
    beta0 = norm1 / norm0
    alpha1 = norm1 / (lane(sums, 1) - beta0 * norm1 / alpha0)
    prod1 = [row_full1, agz_b[:, 0, :], agc_b[...]]
    dir1 = [r1 + beta0 * r0 for r1, r0 in zip(res1, res0)]
    image1 = [d * r + v + beta0 * i for d, r, v, i in zip(diag, res1, prod1, image0)]
    res2 = [r - alpha1 * i for r, i in zip(res1, image1)]
    sol2 = [alpha0 * r0 + alpha1 * d1 for r0, d1 in zip(res0, dir1)]

    row_part = matvec(res2[0], res2[2], False)
    sc_out[...] = scalars(res2, row_part)

    push_all(SW, src_peer, lambda p: sc_out, sc_in.at[s], C_SRC)
    sc_in[s] = sc_out[...]

    vec_t[0:1, :] = jnp.ones((1, NT), F32)
    vec_t[1:2, :] = sol2[2]
    vec_t[2:3, :] = dir1[2]
    vec_t[3:4, :] = res2[2]
    vec_s[:, 0, :] = jnp.ones((ZS, NS), F32)
    vec_s[:, 1, :] = sol2[1]
    vec_s[:, 2, :] = dir1[1]
    vec_s[:, 3, :] = res2[1]

    def fill_stack(points, weights):
        for v in range(VECS):
            weight = weights[v:v + 1, :]
            value = jnp.concatenate([points * weight, jnp.broadcast_to(weight, (16, TILE))], axis=0)
            high, low = halves(value)
            stack[v * STACK:(v + 1) * STACK, :] = high
            stack[(VECS + v) * STACK:(VECS + v + 1) * STACK, :] = low

    def gather_sums(high, low, dims):
        first = lax.dot_general(stack[...], high, (dims, ((), ())), preferred_element_type=F32)
        second = lax.dot_general(
            stack[0:VECS * STACK, :], low, (dims, ((), ())), preferred_element_type=F32
        )
        tsum[...] += first[0:VECS * STACK, :] + first[VECS * STACK:, :] + second

    def gradients(points, own, write):
        ones = tsum[0:64, :], tsum[64:65, :]
        base = points * ones[1] - ones[0]
        for v in range(1, VECS):
            low = v * STACK
            part = points * tsum[low + 64:low + 65, :] - tsum[low:low + 64, :]
            weight = own[v] + 1.0 if v == 1 else own[v]
            write(v - 1, base * weight + part)

    tsum[...] = jnp.zeros_like(tsum)

    def col_step(zz, carry):
        fill_stack(jnp.concatenate([xg[zz, 0], xg[zz, 1]], axis=0), vec_s[zz])
        gather_sums(q_hi[zz], q_lo[zz], ((1,), (0,)))
        return carry
    lax.fori_loop(0, ZS, col_step, 0)

    def write_col(part, value):
        for k in range(XS):
            g_col[part, k] = value[k * 16:(k + 1) * 16, :]
    own_t = vec_t[:, my_tile]
    gradients(ysub[...], [own_t[v:v + 1, :] for v in range(VECS)], write_col)
    push_all(XS, x_peer, lambda p: g_col.at[:, lax.rem(x + p, XS)], g_col_in.at[x], D_COL)
    g_col_in[x] = g_col[:, x]

    wait_in(sc_in.at[pl.ds(0, SW - 1)], C_SRC)
    sc2_out[1] = jnp.sum(sc_in[...], axis=0)
    push_all(TW, tgt_peer, lambda p: sc2_out.at[1], sc2_in.at[t], C_TGT)
    sc2_in[t] = sc2_out[1]

    tsum[...] = jnp.zeros_like(tsum)

    def row_step(n, carry):
        cs = pl.ds(pl.multiple_of(n * TILE, TILE), TILE)
        fill_stack(yt_ref[:, cs], vec_t[:, cs])
        gather_sums(plan_hi[:, cs], plan_lo[:, cs], ((1,), (1,)))
        return carry
    lax.fori_loop(0, NT // TILE, row_step, 0)

    def write_row(part, value):
        for k in range(TW):
            g_row[part, k] = value[k * 8:(k + 1) * 8, :]
    gradients(xs, [None, sol2[0], dir1[0], res2[0]], write_row)
    push_all(TW, tgt_peer, lambda p: g_row.at[:, lax.rem(t + p, TW)], g_row_in.at[t], D_ROW)
    g_row_in[t] = g_row[:, t]

    wait_in(sc2_in.at[pl.ds(0, TW - 1)], C_TGT)
    sums = jnp.sum(sc2_in[...], axis=0)
    norm2 = lane(sums, 0)
    beta1 = norm2 / norm1
    alpha2 = norm2 / (lane(sums, 1) - beta1 * norm2 / alpha1)
    both = alpha2 * beta1

    def combine(parts):
        return (parts[0] + both * parts[1] + alpha2 * parts[2]) * (1.0 / EPSILON)

    wait_in(g_col_in.at[pl.ds(0, XS - 1)], D_COL)
    gt_ref[x, :, my_tile] = combine(jnp.sum(g_col_in[...], axis=0))
    for dx in range(XS):
        def step(p, carry):
            device = (lax.rem(x + dx, XS) * ZS + lax.rem(z + p, ZS), t)
            push(gt_ref.at[x, :, my_tile], gt_ref.at[x, :, my_tile], O_COL, device, O_X + dx)
            return carry
        lax.fori_loop(1 if dx == 0 else 0, ZS, step, 0)

    wait_in(g_row_in.at[pl.ds(0, TW - 1)], D_ROW)
    gs_ref[t] = combine(jnp.sum(g_row_in[...], axis=0))
    push_all(TW, tgt_peer, lambda p: gs_ref.at[t], gs_ref.at[t], O_ROW)

    sol_src_ref[...] = sol2[0] + both * dir1[0] + alpha2 * res2[0]
    sol_tgt_ref[...] = sol2[2] + both * dir1[2] + alpha2 * res2[2]

    wait_in(gs_ref.at[pl.ds(0, TW - 1)], O_ROW)
    wait_in(gt_ref.at[x, :, pl.ds(0, (ZS - 1) * TILE)], O_X)
    for dx in range(1, XS):
        wait_in(gt_ref.at[lax.rem(x + XS - dx, XS)], O_X + dx)

    wait_out(col_a_in.at[pl.ds(0, SW - 1)], A_COL)
    wait_out(row_a_in.at[pl.ds(0, TW - 1)], A_ROW)
    wait_out(init_in.at[pl.ds(0, ZS - 1)], A_INIT)
    wait_out(agc_a.at[:, pl.ds(0, (SW - 1) * SUB)], A_AGC)
    wait_out(agz_a.at[pl.ds(0, ZS - 1)], A_AGZ)
    wait_out(ags_a_in.at[pl.ds(0, TW - 1)], A_AGS)
    wait_out(col_b_in.at[pl.ds(0, SW - 1)], B_COL)
    wait_out(row_b_in.at[pl.ds(0, TW - 1)], B_ROW)
    wait_out(agc_b.at[:, pl.ds(0, (SW - 1) * SUB)], B_AGC)
    wait_out(agz_b.at[pl.ds(0, ZS - 1)], B_AGZ)
    wait_out(ags_b_in.at[pl.ds(0, TW - 1)], B_AGS)
    wait_out(sc_in.at[pl.ds(0, SW - 1)], C_SRC)
    wait_out(sc2_in.at[pl.ds(0, TW - 1)], C_TGT)
    wait_out(g_row_in.at[pl.ds(0, TW - 1)], D_ROW)
    wait_out(g_col_in.at[pl.ds(0, XS - 1)], D_COL)
    wait_out(gs_ref.at[pl.ds(0, TW - 1)], O_ROW)
    wait_out(gt_ref.at[pl.ds(0, 3)], O_COL)
    wait_out(gt_ref.at[0, :, pl.ds(0, (ZS - 1) * TILE)], O_COL)
    wait_out(xg.at[pl.ds(0, 4), 0], G_NEAR)
    wait_out(xg.at[pl.ds(0, 3), 0], G_FAR)
    wait_out(xg.at[pl.ds(0, 4), 0], G_SIB1)
    wait_out(xg.at[pl.ds(0, 3), 0], G_SIB2)


def body(src_points, tgt_points, src_potential, tgt_potential, src_rhs, tgt_rhs):
    normalizer = 1.0 / math.sqrt(NS * SW * NT * TW)
    vmem = pl.BlockSpec(memory_space=pltpu.VMEM)

    def buf(*shape, dtype=F32):
        return pltpu.VMEM(shape, dtype)

    scratch = [
        buf(NS, NT), buf(NS, NT, dtype=BF16), buf(NS, NT, dtype=BF16),
        buf(ZS, NS, TILE, dtype=BF16), buf(ZS, NS, TILE, dtype=BF16),
        buf(NS, 256, dtype=BF16), buf(256, NT, dtype=BF16), buf(NS, TILE),
        buf(NS, 128), buf(NS, 128), buf(NS, 128), buf(NS, 128),
        buf(4, NT), buf(SW, 4, SUB), buf(2, NS), buf(TW, 2, NS),
        buf(2, NS), buf(ZS, 2, NS),
        buf(2, NT), buf(ZS, 2, NS), buf(1, 128), buf(TW, 1, 128),
        buf(2, NT), buf(SW, 2, SUB), buf(1, NS), buf(TW, 1, NS),
        buf(1, NT), buf(ZS, 1, NS), buf(TW, 1, 128),
        buf(1, 128), buf(SW, 1, 128), buf(2, 1, 128), buf(TW, 1, 128),
        buf(DIM, TILE), buf(VECS, NT), buf(ZS, VECS, NS),
        buf(2 * VECS * STACK, TILE, dtype=BF16), buf(VECS * STACK, TILE),
        buf(3, TW, 8, NS), buf(TW, 3, 8, NS),
        buf(3, XS, 16, TILE), buf(XS, 3, 16, TILE),
        buf(ZS, 2, DIM // 2, NS),
        pltpu.SemaphoreType.DMA((N_SEMS,)), pltpu.SemaphoreType.DMA((O_X + XS,)),
    ]
    sol_src, sol_tgt, grad_src, grad_tgt = pl.pallas_call(
        functools.partial(kernel, math.log2(normalizer)),
        out_shape=(
            jax.ShapeDtypeStruct((1, NS), F32),
            jax.ShapeDtypeStruct((1, NT), F32),
            jax.ShapeDtypeStruct((TW, 8, NS), F32),
            jax.ShapeDtypeStruct((XS, 16, NT), F32),
        ),
        in_specs=[vmem] * 6,
        out_specs=[vmem] * 4,
        scratch_shapes=scratch,
        compiler_params=pltpu.CompilerParams(
            collective_id=1, has_side_effects=True, vmem_limit_bytes=56 * 1024 * 1024
        ),
    )(
        src_points.reshape(2, DIM // 2, NS), tgt_points, src_potential.reshape(1, NS),
        tgt_potential.reshape(1, NT), src_rhs.reshape(1, NS), tgt_rhs.reshape(1, NT),
    )
    return (
        sol_src.reshape(NS), sol_tgt.reshape(NT), grad_src.reshape(DIM, NS), grad_tgt.reshape(DIM, NT)
    )


def solution(mesh):
    return jax.shard_map(
        body,
        mesh=mesh,
        in_specs=(P(None, "src"), P(None, "tgt"), P("src"), P("tgt"), P("src"), P("tgt")),
        out_specs=(P("src"), P("tgt"), P(None, "src"), P(None, "tgt")),
        check_vma=False,
    )
```

```python
import functools
import math

import jax
import jax.numpy as jnp
from jax import lax
from jax.experimental import pallas as pl
from jax.experimental.pallas import tpu as pltpu
from jax.sharding import PartitionSpec as P

EPSILON = 0.5
REGULARIZER = 1.0
LOG2E = math.log2(math.e)
MESH = pl.DeviceIdType.MESH
F32 = jnp.float32
BF16 = jnp.bfloat16

XS, ZS = 4, 8
SW, TW = XS * ZS, 8
DIM = 64
NS, NT = 512, 4096
SUB = NT // SW
TILE = 512
STACK = 80
VECS = 4

(A_COL, A_ROW, A_INIT, A_AGC, A_AGZ, A_AGS, B_COL, B_ROW, B_AGC, B_AGZ, B_AGS, C_SRC, C_TGT,
 D_ROW, D_COL, D_ROW2, D_COL2, O_ROW, O_XX, O_XZ, O_ZF, G_NEAR, G_FAR, G_SIB1, G_SIB2) = range(25)
IN_ZF = 25
IN_XF = IN_ZF + ZS
N_SEMS = 25
N_IN = IN_XF + XS
LEAD = 384


def halves(value):
    high = value.astype(BF16)
    return high, (value - high.astype(F32)).astype(BF16)


def across(vector):
    return jnp.broadcast_to(vector, (128, vector.shape[1])).T


def along(block):
    return jnp.sum(block.T, axis=0, keepdims=True)


def tiled(block, times):
    return jnp.concatenate([block] * times, axis=1)


def total(value):
    return jnp.sum(jnp.sum(value, axis=1, keepdims=True), axis=0, keepdims=True)


def lanes(*values):
    spot = lax.broadcasted_iota(jnp.int32, (1, 128), 1)
    row = jnp.zeros((1, 128), F32)
    for index, value in enumerate(values):
        row = row + jnp.where(spot == index, value, 0.0)
    return row


def lane(row, index):
    spot = lax.broadcasted_iota(jnp.int32, (1, 128), 1)
    return jnp.sum(jnp.where(spot == index, row, 0.0), axis=1, keepdims=True)


def kernel(
    shift, xs_hbm, yt_hbm, f_hbm, g_hbm, a0_hbm, b0_hbm,
    sol_src_ref, sol_tgt_ref, gs_ref, gt_ref,
    xs_ref, yt_ref, f_ref, g_ref, a0_ref, b0_ref, load,
    plan, plan_hi, plan_lo, q_hi, q_lo, x4t, y4, fcol, acol, racc, racc2,
    col_a, col_a_in, row_a, row_a_in, init_out, init_in, agc_a, agz_a, ags_a, ags_a_in,
    col_b, col_b_in, row_b, row_b_in, agc_b, agz_b, ags_b_in,
    sc_out, sc_in, sc2_out, sc2_in, ysub, vec_t, vec_s, stack, t_row, t_col,
    g_row, g_row_in, g_col, g_col_in, xg, send, recv,
):
    loads = [
        pltpu.make_async_copy(far, near, load.at[k])
        for k, (far, near) in enumerate((
            (yt_hbm, yt_ref), (xs_hbm, xs_ref), (f_hbm, f_ref), (g_hbm, g_ref), (a0_hbm, a0_ref), (b0_hbm, b0_ref),
        ))
    ]
    for copy in loads:
        copy.start()
    s = lax.axis_index("src")
    t = lax.axis_index("tgt")
    x, z = s // ZS, s % ZS
    core = t % 2
    sibling = (s, t + 1 - 2 * core)

    def src_peer(p):
        return (lax.rem(s + p, SW), t)

    def tgt_peer(p):
        return (s, lax.rem(t + p, TW))

    def z_peer(p):
        return (x * ZS + lax.rem(z + p, ZS), t)

    def x_peer(p):
        return (lax.rem(x + p, XS) * ZS + z, t)

    def push(src, dst, k, device, k_recv=None):
        pltpu.make_async_remote_copy(
            src_ref=src, dst_ref=dst, send_sem=send.at[k],
            recv_sem=recv.at[k if k_recv is None else k_recv],
            device_id=device, device_id_type=MESH,
        ).start()

    def push_all(ways, peer, src, dst, k):
        def step(p, carry):
            push(src(p), dst, k, peer(p))
            return carry
        lax.fori_loop(1, ways, step, 0)

    def wait_in(ref, k):
        pltpu.make_async_copy(ref, ref, recv.at[k]).wait()

    def wait_out(ref, k):
        pltpu.make_async_copy(ref, ref, send.at[k]).wait()

    def sub_of(p):
        return pl.ds(pl.multiple_of(lax.rem(s + p, SW) * SUB, SUB), SUB)

    my_sub = pl.ds(pl.multiple_of(s * SUB, SUB), SUB)
    my_tile = pl.ds(pl.multiple_of(z * TILE, TILE), TILE)

    barrier = pltpu.get_barrier_semaphore()

    def greet(ways, peer):
        def step(p, carry):
            pl.semaphore_signal(barrier, inc=1, device_id=peer(p), device_id_type=MESH)
            return carry
        lax.fori_loop(1, ways, step, 0)

    greet(SW, src_peer)
    greet(TW, tgt_peer)
    for copy in loads:
        copy.wait()

    xs = jnp.concatenate([xs_ref[0], xs_ref[1]], axis=0)
    a0 = a0_ref[...]
    b0 = b0_ref[...]

    def x_parts(points):
        scaled = points * (LOG2E / EPSILON)
        high = scaled.astype(BF16).astype(F32)
        low = scaled - high
        return jnp.concatenate([high, high, low, low], axis=0).T.astype(BF16)

    x4t[...] = x_parts(xs)

    def y_step(n, carry):
        cs = pl.ds(pl.multiple_of(n * TILE, TILE), TILE)
        high, low = halves(yt_ref[:, cs])
        y4[0:64, cs] = high
        y4[64:128, cs] = low
        y4[128:192, cs] = high
        y4[192:256, cs] = low
        return carry
    lax.fori_loop(0, NT // TILE, y_step, 0)

    fcol[...] = across(f_ref[...] * LOG2E + shift)
    acol[...] = across(a0)
    racc[...] = jnp.zeros_like(racc)
    racc2[...] = jnp.zeros_like(racc2)

    def plan_step(n, carry):
        cs = pl.ds(pl.multiple_of(n * TILE, TILE), TILE)
        cross = jnp.dot(x4t[...], y4[:, cs], preferred_element_type=F32)
        g_now = g_ref[:, cs] * LOG2E
        b_now = b0_ref[:, cs]
        mass_sum = jnp.zeros((8, TILE), F32)
        a_sum = jnp.zeros((8, TILE), F32)
        for r in range(0, NS, 64):
            p = jnp.exp2(cross[r:r + 64, :] + tiled(fcol[r:r + 64, :], 4) + g_now)
            plan[r:r + 64, cs] = p
            racc[r:r + 64, :] += (p[:, 0:128] + p[:, 128:256]) + (p[:, 256:384] + p[:, 384:512])
            pb = p * b_now
            racc2[r:r + 64, :] += (pb[:, 0:128] + pb[:, 128:256]) + (pb[:, 256:384] + pb[:, 384:512])
            pa = p * tiled(acol[r:r + 64, :], 4)
            mass_sum = mass_sum + jnp.sum(p.reshape(8, 8, TILE), axis=0)
            a_sum = a_sum + jnp.sum(pa.reshape(8, 8, TILE), axis=0)
        col_a[0:1, cs] = jnp.sum(mass_sum, axis=0, keepdims=True)
        col_a[1:2, cs] = jnp.sum(a_sum, axis=0, keepdims=True)
        return carry
    lax.fori_loop(0, NT // TILE, plan_step, 0)

    mass_part = along(racc[...])
    v_part = along(racc2[...])
    row_a[0:1, :] = mass_part
    row_a[1:2, :] = v_part
    init_out[0:1, :] = f_ref[...]
    init_out[1:2, :] = a0
    norm_part = total(a0 * a0) * (1.0 / TW) + total(b0 * b0) * (1.0 / SW)
    quad_part = (
        norm_part * REGULARIZER
        + total(a0 * a0 * mass_part) + total(b0 * b0 * col_a[0:1, :]) + 2.0 * total(a0 * v_part)
    )
    col_a[2:3, :] = tiled(lanes(norm_part, quad_part), SW)
    col_a[3:4, :] = jnp.zeros((1, NT), F32)

    pl.semaphore_wait(barrier, SW - 1 + TW - 1)

    push_all(SW, src_peer, lambda p: col_a.at[:, sub_of(p)], col_a_in.at[s], A_COL)
    push_all(TW, tgt_peer, lambda p: row_a, row_a_in.at[t], A_ROW)
    push_all(ZS, z_peer, lambda p: init_out, init_in.at[z], A_INIT)
    for p in (1, ZS - 1, 2, ZS - 2):
        push(xs_ref.at[core], xg.at[z, core], G_NEAR, z_peer(p))
    col_a_in[s] = col_a[:, my_sub]
    row_a_in[t] = row_a[...]
    init_in[z] = init_out[...]
    xg[z, 0] = xs_ref[0]
    xg[z, 1] = xs_ref[1]
    ysub[...] = yt_ref[:, my_tile]

    g_sub = g_ref[:, my_tile] * LOG2E

    def q_block(p, carry):
        zz = lax.rem(z + p, ZS)
        points = jnp.concatenate([xg[zz, 0], xg[zz, 1]], axis=0)
        fcol[...] = across(init_in[zz][0:1, :] * LOG2E + shift)
        cross = jnp.dot(x_parts(points), y4[:, my_tile], preferred_element_type=F32)
        for r in range(0, NS, 64):
            value = jnp.exp2(cross[r:r + 64, :] + tiled(fcol[r:r + 64, :], 4) + g_sub)
            high, low = halves(value)
            q_hi[zz, r:r + 64, :] = high
            q_lo[zz, r:r + 64, :] = low
        return carry

    def fill_stack(points, weights):
        count = len(weights)
        for v, weight in enumerate(weights):
            value = jnp.concatenate([points * weight, jnp.broadcast_to(weight, (16, TILE))], axis=0)
            high, low = halves(value)
            stack[v * STACK:(v + 1) * STACK, :] = high
            stack[(count + v) * STACK:(count + v + 1) * STACK, :] = low

    def add_sums(out, low, count, plan_high, plan_low, dims):
        rows = count * STACK
        first = lax.dot_general(
            stack[0:2 * rows, :], plan_high, (dims, ((), ())), preferred_element_type=F32
        )
        second = lax.dot_general(
            stack[0:rows, :], plan_low, (dims, ((), ())), preferred_element_type=F32
        )
        out[low * STACK:low * STACK + rows, :] += first[0:rows, :] + first[rows:, :] + second

    def row_sums(low, high, split=False):
        def step(n, carry):
            cs = pl.ds(pl.multiple_of(n * TILE, TILE), TILE)
            if split:
                for r in range(0, NS, 64):
                    top, rest = halves(plan[r:r + 64, cs])
                    plan_hi[r:r + 64, cs] = top
                    plan_lo[r:r + 64, cs] = rest
            fill_stack(yt_ref[:, cs], [vec_t[v:v + 1, cs] for v in range(low, high)])
            add_sums(t_row, low, high - low, plan_hi[:, cs], plan_lo[:, cs], ((1,), (1,)))
            return carry
        lax.fori_loop(0, NT // TILE, step, 0)

    def col_sums(low, high):
        def step(zz, carry):
            fill_stack(
                jnp.concatenate([xg[zz, 0], xg[zz, 1]], axis=0),
                [vec_s[zz, v:v + 1, :] for v in range(low, high)],
            )
            add_sums(t_col, low, high - low, q_hi[zz], q_lo[zz], ((1,), (0,)))
            return carry
        lax.fori_loop(0, ZS, step, 0)

    t_row[...] = jnp.zeros_like(t_row)
    t_col[...] = jnp.zeros_like(t_col)
    vec_t[0:1, :] = jnp.ones((1, NT), F32)
    vec_t[1:2, :] = b0
    vec_s[:, 0, :] = jnp.ones((ZS, NS), F32)
    row_sums(0, 2, split=True)

    wait_in(row_a_in.at[pl.ds(0, TW - 1)], A_ROW)
    row_full = jnp.sum(row_a_in[...], axis=0)
    agz_own = row_full
    wait_in(col_a_in.at[pl.ds(0, SW - 1)], A_COL)
    col_full = jnp.sum(col_a_in[...], axis=0)
    agc_a[:, my_sub] = col_full[0:2, :]
    ags_a[...] = col_full[2:3, :]
    agz_a[z] = agz_own

    push_all(SW, src_peer, lambda p: agc_a.at[:, my_sub], agc_a.at[:, my_sub], A_AGC)
    push_all(TW, tgt_peer, lambda p: ags_a, ags_a_in.at[t], A_AGS)
    push_all(ZS, z_peer, lambda p: agz_a.at[z], agz_a.at[z], A_AGZ)
    ags_a_in[t] = ags_a[...]
    wait_in(init_in.at[pl.ds(0, ZS - 1)], A_INIT)
    wait_in(xg.at[pl.ds(0, 4), 0], G_NEAR)
    for p in (1, ZS - 1, 2, ZS - 2):
        zz = lax.rem(z + p, ZS)
        push(xg.at[zz, core], xg.at[zz, core], G_SIB1, sibling)
    for p in (3, ZS - 3, 4):
        push(xs_ref.at[core], xg.at[z, core], G_FAR, z_peer(p))
    q_block(0, 0)
    wait_in(xg.at[pl.ds(0, 4), 0], G_SIB1)
    lax.fori_loop(1, 3, q_block, 0)
    lax.fori_loop(6, 8, q_block, 0)

    wait_in(agz_a.at[pl.ds(0, ZS - 1)], A_AGZ)
    wait_in(ags_a_in.at[pl.ds(0, TW - 1)], A_AGS)
    wait_in(agc_a.at[:, pl.ds(0, (SW - 1) * SUB)], A_AGC)
    sums = jnp.sum(ags_a_in[...], axis=0)
    norm0 = lane(sums, 0)
    alpha0 = norm0 / lane(sums, 1)

    diag = [row_full[0:1, :] + REGULARIZER, agz_a[:, 0, :] + REGULARIZER, agc_a[0:1, :] + REGULARIZER]
    res0 = [a0, init_in[:, 1, :], b0]
    prod0 = [row_full[1:2, :], agz_a[:, 1, :], agc_a[1:2, :]]
    image0 = [d * r + v for d, r, v in zip(diag, res0, prod0)]
    res1 = [r - alpha0 * i for r, i in zip(res0, image0)]

    def matvec(vec_src, vec_tgt, columns):
        acol[...] = across(vec_src)
        half = NT // 2
        for h, acc in ((0, racc), (1, racc2)):
            spread = jnp.broadcast_to(vec_tgt[:, h * half:(h + 1) * half], (8, half))

            def step(r, sums):
                rows = pl.ds(pl.multiple_of(r * 8, 8), 8)
                p = plan[rows, h * half:(h + 1) * half]
                terms = p * spread
                parts = [terms[:, k * 128:(k + 1) * 128] for k in range(half // 128)]
                while len(parts) > 1:
                    parts = [parts[k] + parts[k + 1] for k in range(0, len(parts), 2)]
                acc[rows, :] = parts[0]
                if columns:
                    sums = sums + p * tiled(acol[rows, :], half // 128)
                return sums
            sums = lax.fori_loop(0, NS // 8, step, jnp.zeros((8, half), F32), unroll=2)
            if columns:
                col_b[0:1, h * half:(h + 1) * half] = jnp.sum(sums, axis=0, keepdims=True)
        return along(racc[...] + racc2[...])

    def scalars(res, row_part):
        norm = total(res[0] * res[0]) * (1.0 / TW) + total(res[2] * res[2]) * (1.0 / SW)
        quad = (
            total(res[0] * res[0] * diag[0]) * (1.0 / TW)
            + total(res[2] * res[2] * diag[2]) * (1.0 / SW)
            + 2.0 * total(res[0] * row_part)
        )
        return lanes(norm, quad)

    row_part = matvec(res1[0], res1[2], True)
    row_b[...] = row_part
    col_b[1:2, :] = tiled(scalars(res1, row_part), SW)

    push_all(SW, src_peer, lambda p: col_b.at[:, sub_of(p)], col_b_in.at[s], B_COL)
    push_all(TW, tgt_peer, lambda p: row_b, row_b_in.at[t], B_ROW)
    col_b_in[s] = col_b[:, my_sub]
    row_b_in[t] = row_b[...]
    wait_in(xg.at[pl.ds(0, 3), 0], G_FAR)
    for p in (3, ZS - 3, 4):
        zz = lax.rem(z + p, ZS)
        push(xg.at[zz, core], xg.at[zz, core], G_SIB2, sibling)
    vec_t[2:3, :] = res1[2]
    vec_s[:, 1, :] = res0[1]
    vec_s[:, 2, :] = res1[1]
    row_sums(2, 3)
    wait_in(xg.at[pl.ds(0, 3), 0], G_SIB2)
    lax.fori_loop(3, 6, q_block, 0)

    wait_in(row_b_in.at[pl.ds(0, TW - 1)], B_ROW)
    row_full1 = jnp.sum(row_b_in[...], axis=0)
    agz_b[z] = row_full1
    wait_in(col_b_in.at[pl.ds(0, SW - 1)], B_COL)
    col_full1 = jnp.sum(col_b_in[...], axis=0)
    agc_b[:, my_sub] = col_full1[0:1, :]
    sc2_out[0] = col_full1[1:2, :]

    push_all(SW, src_peer, lambda p: agc_b.at[:, my_sub], agc_b.at[:, my_sub], B_AGC)
    push_all(TW, tgt_peer, lambda p: sc2_out.at[0], ags_b_in.at[t], B_AGS)
    push_all(ZS, z_peer, lambda p: agz_b.at[z], agz_b.at[z], B_AGZ)
    ags_b_in[t] = sc2_out[0]
    col_sums(0, 3)

    wait_in(agz_b.at[pl.ds(0, ZS - 1)], B_AGZ)
    wait_in(ags_b_in.at[pl.ds(0, TW - 1)], B_AGS)
    wait_in(agc_b.at[:, pl.ds(0, (SW - 1) * SUB)], B_AGC)
    sums = jnp.sum(ags_b_in[...], axis=0)
    norm1 = lane(sums, 0)
    beta0 = norm1 / norm0
    alpha1 = norm1 / (lane(sums, 1) - beta0 * norm1 / alpha0)
    prod1 = [row_full1, agz_b[:, 0, :], agc_b[...]]
    dir1 = [r1 + beta0 * r0 for r1, r0 in zip(res1, res0)]
    image1 = [d * r + v + beta0 * i for d, r, v, i in zip(diag, res1, prod1, image0)]
    res2 = [r - alpha1 * i for r, i in zip(res1, image1)]
    sol2 = [alpha0 * r0 + alpha1 * d1 for r0, d1 in zip(res0, dir1)]

    row_part = matvec(res2[0], res2[2], False)
    sc_out[...] = scalars(res2, row_part)

    push_all(SW, src_peer, lambda p: sc_out, sc_in.at[s], C_SRC)
    sc_in[s] = sc_out[...]

    vec_t[3:4, :] = res2[2]
    vec_s[:, 3, :] = res2[1]
    first_step = alpha0 + alpha1 * beta0

    def sums_of(points, out, v):
        low = v * STACK
        return points * out[low + 64:low + 65, :] - out[low:low + 64, :]

    def early_gradients(points, out, own, write):
        ones = sums_of(points, out, 0)
        zeroth = sums_of(points, out, 1)
        latest = sums_of(points, out, 2)
        write(0, (1.0 + first_step * own[0] + alpha1 * own[1]) * ones + first_step * zeroth + alpha1 * latest)
        write(1, (own[1] + beta0 * own[0]) * ones + latest + beta0 * zeroth)

    def late_gradient(points, out, own, write):
        write(2, own[2] * sums_of(points, out, 0) + sums_of(points, out, 3))

    def write_col(part, value):
        for k in range(XS):
            g_col[part, k] = value[k * 16:(k + 1) * 16, :]

    def write_row(part, value):
        for k in range(TW):
            g_row[part, k] = value[k * 8:(k + 1) * 8, :]

    early, late = pl.ds(0, 2), pl.ds(2, 1)
    own_t = vec_t[:, my_tile]
    own_t = [own_t[v:v + 1, :] for v in range(1, VECS)]
    own_s = [res0[0], res1[0], res2[0]]
    early_gradients(ysub[...], t_col, own_t, write_col)
    push_all(XS, x_peer, lambda p: g_col.at[early, lax.rem(x + p, XS)], g_col_in.at[x, early], D_COL)
    early_gradients(xs, t_row, own_s, write_row)
    push_all(TW, tgt_peer, lambda p: g_row.at[early, lax.rem(t + p, TW)], g_row_in.at[t, early], D_ROW)
    col_sums(3, 4)
    late_gradient(ysub[...], t_col, own_t, write_col)
    push_all(XS, x_peer, lambda p: g_col.at[late, lax.rem(x + p, XS)], g_col_in.at[x, late], D_COL2)
    g_col_in[x] = g_col[:, x]
    row_sums(3, 4)
    late_gradient(xs, t_row, own_s, write_row)
    push_all(TW, tgt_peer, lambda p: g_row.at[late, lax.rem(t + p, TW)], g_row_in.at[t, late], D_ROW2)
    g_row_in[t] = g_row[:, t]

    wait_in(sc_in.at[pl.ds(0, SW - 1)], C_SRC)
    sc2_out[1] = jnp.sum(sc_in[...], axis=0)
    push_all(TW, tgt_peer, lambda p: sc2_out.at[1], sc2_in.at[t], C_TGT)
    sc2_in[t] = sc2_out[1]

    wait_in(sc2_in.at[pl.ds(0, TW - 1)], C_TGT)
    sums = jnp.sum(sc2_in[...], axis=0)
    norm2 = lane(sums, 0)
    beta1 = norm2 / norm1
    alpha2 = norm2 / (lane(sums, 1) - beta1 * norm2 / alpha1)
    both = alpha2 * beta1

    def combine(parts):
        return (parts[0] + both * parts[1] + alpha2 * parts[2]) * (1.0 / EPSILON)

    def lead_of(zz):
        return pl.ds(pl.multiple_of(zz * TILE, TILE), LEAD)

    def rest_of(zz):
        return pl.ds(pl.multiple_of(zz * TILE + LEAD, 128), TILE - LEAD)

    wait_in(g_col_in.at[pl.ds(0, XS - 1), early], D_COL)
    wait_in(g_col_in.at[pl.ds(0, XS - 1), late], D_COL2)
    gt_ref[x, :, my_tile] = combine(jnp.sum(g_col_in[...], axis=0))
    mine = gt_ref.at[x, :, rest_of(z)]
    push_all(XS, x_peer, lambda p: mine, mine, O_XX)
    for p in (4, 3, ZS - 3, 2, ZS - 2, 1, ZS - 1):
        push(gt_ref.at[x, :, lead_of(z)], gt_ref.at[x, :, lead_of(z)], O_ZF, z_peer(p), IN_ZF + p)

    def lead_along_x(zz):
        for p in range(1, XS):
            push(gt_ref.at[x, :, lead_of(zz)], gt_ref.at[x, :, lead_of(zz)], O_ZF, x_peer(p), IN_XF + p)

    lead_along_x(z)

    wait_in(g_row_in.at[pl.ds(0, TW - 1), early], D_ROW)
    wait_in(g_row_in.at[pl.ds(0, TW - 1), late], D_ROW2)
    gs_ref[t] = combine(jnp.sum(g_row_in[...], axis=0))
    push_all(TW, tgt_peer, lambda p: gs_ref.at[t], gs_ref.at[t], O_ROW)

    sol_src_ref[...] = sol2[0] + both * dir1[0] + alpha2 * res2[0]
    sol_tgt_ref[...] = sol2[2] + both * dir1[2] + alpha2 * res2[2]

    wait_in(gt_ref.at[pl.ds(0, XS - 1), :, pl.ds(0, TILE - LEAD)], O_XX)
    push_all(
        ZS, z_peer, lambda p: gt_ref.at[:, :, rest_of(z)], gt_ref.at[:, :, rest_of(z)], O_XZ
    )
    for p in (1, ZS - 1, 2, ZS - 2, 3, ZS - 3, 4):
        zz = lax.rem(z + ZS - p, ZS)
        wait_in(gt_ref.at[x, :, lead_of(zz)], IN_ZF + p)
        lead_along_x(zz)

    wait_in(gs_ref.at[pl.ds(0, TW - 1)], O_ROW)
    wait_in(gt_ref.at[:, :, pl.ds(0, (ZS - 1) * (TILE - LEAD))], O_XZ)
    for p in range(1, XS):
        wait_in(gt_ref.at[0, :, pl.ds(0, ZS * LEAD)], IN_XF + p)

    wait_out(col_a_in.at[pl.ds(0, SW - 1)], A_COL)
    wait_out(row_a_in.at[pl.ds(0, TW - 1)], A_ROW)
    wait_out(init_in.at[pl.ds(0, ZS - 1)], A_INIT)
    wait_out(agc_a.at[:, pl.ds(0, (SW - 1) * SUB)], A_AGC)
    wait_out(agz_a.at[pl.ds(0, ZS - 1)], A_AGZ)
    wait_out(ags_a_in.at[pl.ds(0, TW - 1)], A_AGS)
    wait_out(col_b_in.at[pl.ds(0, SW - 1)], B_COL)
    wait_out(row_b_in.at[pl.ds(0, TW - 1)], B_ROW)
    wait_out(agc_b.at[:, pl.ds(0, (SW - 1) * SUB)], B_AGC)
    wait_out(agz_b.at[pl.ds(0, ZS - 1)], B_AGZ)
    wait_out(ags_b_in.at[pl.ds(0, TW - 1)], B_AGS)
    wait_out(sc_in.at[pl.ds(0, SW - 1)], C_SRC)
    wait_out(sc2_in.at[pl.ds(0, TW - 1)], C_TGT)
    wait_out(g_row_in.at[pl.ds(0, TW - 1), early], D_ROW)
    wait_out(g_col_in.at[pl.ds(0, XS - 1), early], D_COL)
    wait_out(g_row_in.at[pl.ds(0, TW - 1), late], D_ROW2)
    wait_out(g_col_in.at[pl.ds(0, XS - 1), late], D_COL2)
    wait_out(gs_ref.at[pl.ds(0, TW - 1)], O_ROW)
    wait_out(gt_ref.at[pl.ds(0, XS - 1), :, pl.ds(0, TILE - LEAD)], O_XX)
    wait_out(gt_ref.at[:, :, pl.ds(0, (ZS - 1) * (TILE - LEAD))], O_XZ)
    wait_out(gt_ref.at[pl.ds(0, 3), :, pl.ds(0, ZS * LEAD)], O_ZF)
    wait_out(gt_ref.at[0, :, pl.ds(0, (ZS - 1) * LEAD)], O_ZF)
    wait_out(xg.at[pl.ds(0, 4), 0], G_NEAR)
    wait_out(xg.at[pl.ds(0, 3), 0], G_FAR)
    wait_out(xg.at[pl.ds(0, 4), 0], G_SIB1)
    wait_out(xg.at[pl.ds(0, 3), 0], G_SIB2)


def hand_out(*refs):
    count = len(refs) // 2
    sems = refs[-1]
    copies = [pltpu.make_async_copy(refs[k], refs[count + k], sems.at[k]) for k in range(count)]
    for copy in copies:
        copy.start()
    for copy in copies:
        copy.wait()


def body(src_points, tgt_points, src_potential, tgt_potential, src_rhs, tgt_rhs):
    normalizer = 1.0 / math.sqrt(NS * SW * NT * TW)
    vmem = pl.BlockSpec(memory_space=pltpu.VMEM)
    far = pl.BlockSpec(memory_space=pltpu.HBM)

    def buf(*shape, dtype=F32):
        return pltpu.VMEM(shape, dtype)

    scratch = [
        buf(2, DIM // 2, NS), buf(DIM, NT), buf(1, NS), buf(1, NT), buf(1, NS), buf(1, NT),
        pltpu.SemaphoreType.DMA((6,)),
        buf(NS, NT), buf(NS, NT, dtype=BF16), buf(NS, NT, dtype=BF16),
        buf(ZS, NS, TILE, dtype=BF16), buf(ZS, NS, TILE, dtype=BF16),
        buf(NS, 256, dtype=BF16), buf(256, NT, dtype=BF16),
        buf(NS, 128), buf(NS, 128), buf(NS, 128), buf(NS, 128),
        buf(4, NT), buf(SW, 4, SUB), buf(2, NS), buf(TW, 2, NS),
        buf(2, NS), buf(ZS, 2, NS),
        buf(2, NT), buf(ZS, 2, NS), buf(1, 128), buf(TW, 1, 128),
        buf(2, NT), buf(SW, 2, SUB), buf(1, NS), buf(TW, 1, NS),
        buf(1, NT), buf(ZS, 1, NS), buf(TW, 1, 128),
        buf(1, 128), buf(SW, 1, 128), buf(2, 1, 128), buf(TW, 1, 128),
        buf(DIM, TILE), buf(VECS, NT), buf(ZS, VECS, NS),
        buf(2 * 3 * STACK, TILE, dtype=BF16),
        buf(VECS * STACK, NS), buf(VECS * STACK, TILE),
        buf(3, TW, 8, NS), buf(TW, 3, 8, NS),
        buf(3, XS, 16, TILE), buf(XS, 3, 16, TILE),
        buf(ZS, 2, DIM // 2, NS),
        pltpu.SemaphoreType.DMA((N_SEMS,)), pltpu.SemaphoreType.DMA((N_IN,)),
    ]
    shapes = (
        jax.ShapeDtypeStruct((1, NS), F32),
        jax.ShapeDtypeStruct((1, NT), F32),
        jax.ShapeDtypeStruct((TW, 8, NS), F32),
        jax.ShapeDtypeStruct((XS, 16, NT), F32),
    )
    results = pl.pallas_call(
        functools.partial(kernel, math.log2(normalizer)),
        out_shape=shapes,
        in_specs=[far] * 6,
        out_specs=[vmem] * 4,
        scratch_shapes=scratch,
        compiler_params=pltpu.CompilerParams(
            collective_id=1, has_side_effects=True, vmem_limit_bytes=60 * 1024 * 1024
        ),
    )(
        src_points.reshape(2, DIM // 2, NS), tgt_points, src_potential.reshape(1, NS),
        tgt_potential.reshape(1, NT), src_rhs.reshape(1, NS), tgt_rhs.reshape(1, NT),
    )
    sol_src, sol_tgt, grad_src, grad_tgt = pl.pallas_call(
        hand_out,
        out_shape=shapes,
        in_specs=[vmem] * 4,
        out_specs=[far] * 4,
        scratch_shapes=[pltpu.SemaphoreType.DMA((4,))],
    )(*results)
    return (
        sol_src.reshape(NS), sol_tgt.reshape(NT), grad_src.reshape(DIM, NS), grad_tgt.reshape(DIM, NT)
    )


def solution(mesh):
    return jax.shard_map(
        body,
        mesh=mesh,
        in_specs=(P(None, "src"), P(None, "tgt"), P("src"), P("tgt"), P("src"), P("tgt")),
        out_specs=(P("src"), P("tgt"), P(None, "src"), P(None, "tgt")),
        check_vma=False,
    )
```

```python
import functools
import math

import jax
import jax.numpy as jnp
from jax import lax
from jax.experimental import pallas as pl
from jax.experimental.pallas import tpu as pltpu
from jax.sharding import PartitionSpec as P

EPSILON = 0.5
REGULARIZER = 1.0
LOG2E = math.log2(math.e)
MESH = pl.DeviceIdType.MESH
F32 = jnp.float32
BF16 = jnp.bfloat16

XS, ZS = 4, 8
SW, TW = XS * ZS, 8
DIM = 64
NS, NT = 512, 4096
SUB = NT // SW
TILE = 512
STACK = 80
VECS = 4

(A_COL, A_ROW, A_INIT, A_AGC, A_AGZ, A_AGS, B_COL, B_ROW, B_AGC, B_AGZ, B_AGS, C_SRC, C_TGT,
 D_ROW, D_COL, D_ROW2, D_COL2, O_ROW, O_XX, O_XZ, O_ZF, G_RING1, G_RING2, G_RING3, G_RING4, G_SIB1, G_SIB2) = range(27)
IN_ZF = 27
IN_XF = IN_ZF + ZS
N_SEMS = 27
N_IN = IN_XF + XS
LEAD = 384


def halves(value):
    high = value.astype(BF16)
    return high, (value - high.astype(F32)).astype(BF16)


def across(vector):
    return jnp.broadcast_to(vector, (128, vector.shape[1])).T


def along(block):
    return jnp.sum(block.T, axis=0, keepdims=True)


def tiled(block, times):
    return jnp.concatenate([block] * times, axis=1)


def total(value):
    return jnp.sum(jnp.sum(value, axis=1, keepdims=True), axis=0, keepdims=True)


def lanes(*values):
    spot = lax.broadcasted_iota(jnp.int32, (1, 128), 1)
    row = jnp.zeros((1, 128), F32)
    for index, value in enumerate(values):
        row = row + jnp.where(spot == index, value, 0.0)
    return row


def lane(row, index):
    spot = lax.broadcasted_iota(jnp.int32, (1, 128), 1)
    return jnp.sum(jnp.where(spot == index, row, 0.0), axis=1, keepdims=True)


def kernel(
    shift, xs_hbm, yt_hbm, f_hbm, g_hbm, a0_hbm, b0_hbm,
    sol_src_ref, sol_tgt_ref, gs_ref, gt_ref,
    xs_ref, yt_ref, f_ref, g_ref, a0_ref, b0_ref, load,
    plan, plan_hi, plan_lo, q_hi, q_lo, x4t, y4, fcol, acol, racc, racc2,
    col_a, col_a_in, row_a, row_a_in, init_out, init_in, agc_a, agz_a, ags_a, ags_a_in,
    col_b, col_b_in, row_b, row_b_in, agc_b, agz_b, ags_b_in,
    sc_out, sc_in, sc2_out, sc2_in, ysub, vec_t, vec_s, stack, t_row, t_col,
    g_row, g_row_in, g_col, g_col_in, xg, send, recv,
):
    loads = [
        pltpu.make_async_copy(far, near, load.at[k])
        for k, (far, near) in enumerate((
            (yt_hbm, yt_ref), (xs_hbm, xs_ref), (f_hbm, f_ref), (g_hbm, g_ref), (a0_hbm, a0_ref), (b0_hbm, b0_ref),
        ))
    ]
    for copy in loads:
        copy.start()
    s = lax.axis_index("src")
    t = lax.axis_index("tgt")
    x, z = s // ZS, s % ZS
    core = t % 2
    sibling = (s, t + 1 - 2 * core)

    def src_peer(p):
        return (lax.rem(s + p, SW), t)

    def tgt_peer(p):
        return (s, lax.rem(t + p, TW))

    def z_peer(p):
        return (x * ZS + lax.rem(z + p, ZS), t)

    def x_peer(p):
        return (lax.rem(x + p, XS) * ZS + z, t)

    def push(src, dst, k, device, k_recv=None):
        pltpu.make_async_remote_copy(
            src_ref=src, dst_ref=dst, send_sem=send.at[k],
            recv_sem=recv.at[k if k_recv is None else k_recv],
            device_id=device, device_id_type=MESH,
        ).start()

    def push_all(ways, peer, src, dst, k):
        def step(p, carry):
            push(src(p), dst, k, peer(p))
            return carry
        lax.fori_loop(1, ways, step, 0)

    def wait_in(ref, k):
        pltpu.make_async_copy(ref, ref, recv.at[k]).wait()

    def wait_out(ref, k):
        pltpu.make_async_copy(ref, ref, send.at[k]).wait()

    def sub_of(p):
        return pl.ds(pl.multiple_of(lax.rem(s + p, SW) * SUB, SUB), SUB)

    my_sub = pl.ds(pl.multiple_of(s * SUB, SUB), SUB)
    my_tile = pl.ds(pl.multiple_of(z * TILE, TILE), TILE)

    barrier = pltpu.get_barrier_semaphore()

    def greet(ways, peer):
        def step(p, carry):
            pl.semaphore_signal(barrier, inc=1, device_id=peer(p), device_id_type=MESH)
            return carry
        lax.fori_loop(1, ways, step, 0)

    greet(SW, src_peer)
    greet(TW, tgt_peer)
    for copy in loads[1:]:
        copy.wait()

    xs = jnp.concatenate([xs_ref[0], xs_ref[1]], axis=0)
    a0 = a0_ref[...]
    b0 = b0_ref[...]

    def x_parts(points):
        scaled = points * (LOG2E / EPSILON)
        high = scaled.astype(BF16).astype(F32)
        low = scaled - high
        return jnp.concatenate([high, high, low, low], axis=0).T.astype(BF16)

    x4t[...] = x_parts(xs)

    fcol[...] = across(f_ref[...] * LOG2E + shift)
    acol[...] = across(a0)
    racc[...] = jnp.zeros_like(racc)
    racc2[...] = jnp.zeros_like(racc2)

    loads[0].wait()

    def plan_step(n, carry):
        cs = pl.ds(pl.multiple_of(n * TILE, TILE), TILE)
        high, low = halves(yt_ref[:, cs])
        y4[0:64, cs] = high
        y4[64:128, cs] = low
        y4[128:192, cs] = high
        y4[192:256, cs] = low
        cross = jnp.dot(
            x4t[...], jnp.concatenate([high, low, high, low], axis=0), preferred_element_type=F32
        )
        g_now = g_ref[:, cs] * LOG2E
        b_now = b0_ref[:, cs]
        mass_sum = jnp.zeros((8, TILE), F32)
        a_sum = jnp.zeros((8, TILE), F32)
        for r in range(0, NS, 64):
            p = jnp.exp2(cross[r:r + 64, :] + tiled(fcol[r:r + 64, :], 4) + g_now)
            plan[r:r + 64, cs] = p
            racc[r:r + 64, :] += (p[:, 0:128] + p[:, 128:256]) + (p[:, 256:384] + p[:, 384:512])
            pb = p * b_now
            racc2[r:r + 64, :] += (pb[:, 0:128] + pb[:, 128:256]) + (pb[:, 256:384] + pb[:, 384:512])
            pa = p * tiled(acol[r:r + 64, :], 4)
            mass_sum = mass_sum + jnp.sum(p.reshape(8, 8, TILE), axis=0)
            a_sum = a_sum + jnp.sum(pa.reshape(8, 8, TILE), axis=0)
        col_a[0:1, cs] = jnp.sum(mass_sum, axis=0, keepdims=True)
        col_a[1:2, cs] = jnp.sum(a_sum, axis=0, keepdims=True)
        return carry
    lax.fori_loop(0, NT // TILE, plan_step, 0)

    mass_part = along(racc[...])
    v_part = along(racc2[...])
    row_a[0:1, :] = mass_part
    row_a[1:2, :] = v_part
    init_out[0:1, :] = f_ref[...]
    init_out[1:2, :] = a0
    norm_part = total(a0 * a0) * (1.0 / TW) + total(b0 * b0) * (1.0 / SW)
    quad_part = (
        norm_part * REGULARIZER
        + total(a0 * a0 * mass_part) + total(b0 * b0 * col_a[0:1, :]) + 2.0 * total(a0 * v_part)
    )
    col_a[2:3, :] = tiled(lanes(norm_part, quad_part), SW)
    col_a[3:4, :] = jnp.zeros((1, NT), F32)

    pl.semaphore_wait(barrier, SW - 1 + TW - 1)

    push_all(SW, src_peer, lambda p: col_a.at[:, sub_of(p)], col_a_in.at[s], A_COL)
    push_all(TW, tgt_peer, lambda p: row_a, row_a_in.at[t], A_ROW)
    push_all(ZS, z_peer, lambda p: init_out, init_in.at[z], A_INIT)
    push(xs_ref.at[core], xg.at[z, core], G_RING1, z_peer(1))
    push(xs_ref.at[core], xg.at[z, core], G_RING1, z_peer(ZS - 1))
    col_a_in[s] = col_a[:, my_sub]
    row_a_in[t] = row_a[...]
    init_in[z] = init_out[...]
    xg[z, 0] = xs_ref[0]
    xg[z, 1] = xs_ref[1]
    ysub[...] = yt_ref[:, my_tile]

    g_sub = g_ref[:, my_tile] * LOG2E

    def q_block(p, carry):
        zz = lax.rem(z + p, ZS)
        points = jnp.concatenate([xg[zz, 0], xg[zz, 1]], axis=0)
        fcol[...] = across(init_in[zz][0:1, :] * LOG2E + shift)
        cross = jnp.dot(x_parts(points), y4[:, my_tile], preferred_element_type=F32)
        for r in range(0, NS, 64):
            value = jnp.exp2(cross[r:r + 64, :] + tiled(fcol[r:r + 64, :], 4) + g_sub)
            high, low = halves(value)
            q_hi[zz, r:r + 64, :] = high
            q_lo[zz, r:r + 64, :] = low
        return carry

    def pass_on(p, k):
        before, after = lax.rem(z + ZS - p, ZS), lax.rem(z + p, ZS)
        push(xg.at[before, core], xg.at[before, core], k, z_peer(1))
        push(xg.at[after, core], xg.at[after, core], k, z_peer(ZS - 1))

    def fill_stack(points, weights):
        count = len(weights)
        for v, weight in enumerate(weights):
            value = jnp.concatenate([points * weight, jnp.broadcast_to(weight, (16, TILE))], axis=0)
            high, low = halves(value)
            stack[v * STACK:(v + 1) * STACK, :] = high
            stack[(count + v) * STACK:(count + v + 1) * STACK, :] = low

    def add_sums(out, low, count, plan_high, plan_low, dims):
        rows = count * STACK
        first = lax.dot_general(
            stack[0:2 * rows, :], plan_high, (dims, ((), ())), preferred_element_type=F32
        )
        second = lax.dot_general(
            stack[0:rows, :], plan_low, (dims, ((), ())), preferred_element_type=F32
        )
        out[low * STACK:low * STACK + rows, :] += first[0:rows, :] + first[rows:, :] + second

    def row_sums(low, high, split=False):
        def step(n, carry):
            cs = pl.ds(pl.multiple_of(n * TILE, TILE), TILE)
            if split:
                for r in range(0, NS, 64):
                    top, rest = halves(plan[r:r + 64, cs])
                    plan_hi[r:r + 64, cs] = top
                    plan_lo[r:r + 64, cs] = rest
            fill_stack(yt_ref[:, cs], [vec_t[v:v + 1, cs] for v in range(low, high)])
            add_sums(t_row, low, high - low, plan_hi[:, cs], plan_lo[:, cs], ((1,), (1,)))
            return carry
        lax.fori_loop(0, NT // TILE, step, 0)

    def col_sums(low, high, first=0, last=ZS):
        def step(p, carry):
            zz = lax.rem(z + p, ZS)
            fill_stack(
                jnp.concatenate([xg[zz, 0], xg[zz, 1]], axis=0),
                [vec_s[zz, v:v + 1, :] for v in range(low, high)],
            )
            add_sums(t_col, low, high - low, q_hi[zz], q_lo[zz], ((1,), (0,)))
            return carry
        lax.fori_loop(first, last, step, 0)

    t_row[...] = jnp.zeros_like(t_row)
    t_col[...] = jnp.zeros_like(t_col)
    vec_t[0:1, :] = jnp.ones((1, NT), F32)
    vec_t[1:2, :] = b0
    vec_s[:, 0, :] = jnp.ones((ZS, NS), F32)
    row_sums(0, 2, split=True)
    wait_in(xg.at[pl.ds(0, 2), 0], G_RING1)
    pass_on(1, G_RING2)

    wait_in(row_a_in.at[pl.ds(0, TW - 1)], A_ROW)
    row_full = jnp.sum(row_a_in[...], axis=0)
    agz_own = row_full
    wait_in(col_a_in.at[pl.ds(0, SW - 1)], A_COL)
    col_full = jnp.sum(col_a_in[...], axis=0)
    agc_a[:, my_sub] = col_full[0:2, :]
    ags_a[...] = col_full[2:3, :]
    agz_a[z] = agz_own

    push_all(SW, src_peer, lambda p: agc_a.at[:, my_sub], agc_a.at[:, my_sub], A_AGC)
    push_all(TW, tgt_peer, lambda p: ags_a, ags_a_in.at[t], A_AGS)
    push_all(ZS, z_peer, lambda p: agz_a.at[z], agz_a.at[z], A_AGZ)
    ags_a_in[t] = ags_a[...]
    wait_in(init_in.at[pl.ds(0, ZS - 1)], A_INIT)
    wait_in(xg.at[pl.ds(0, 2), 0], G_RING2)
    pass_on(2, G_RING3)
    for p in (1, ZS - 1, 2, ZS - 2):
        zz = lax.rem(z + p, ZS)
        push(xg.at[zz, core], xg.at[zz, core], G_SIB1, sibling)
    q_block(0, 0)
    wait_in(xg.at[pl.ds(0, 4), 0], G_SIB1)
    lax.fori_loop(1, 3, q_block, 0)
    lax.fori_loop(6, 8, q_block, 0)

    wait_in(agz_a.at[pl.ds(0, ZS - 1)], A_AGZ)
    wait_in(ags_a_in.at[pl.ds(0, TW - 1)], A_AGS)
    wait_in(agc_a.at[:, pl.ds(0, (SW - 1) * SUB)], A_AGC)
    sums = jnp.sum(ags_a_in[...], axis=0)
    norm0 = lane(sums, 0)
    alpha0 = norm0 / lane(sums, 1)

    diag = [row_full[0:1, :] + REGULARIZER, agz_a[:, 0, :] + REGULARIZER, agc_a[0:1, :] + REGULARIZER]
    res0 = [a0, init_in[:, 1, :], b0]
    prod0 = [row_full[1:2, :], agz_a[:, 1, :], agc_a[1:2, :]]
    image0 = [d * r + v for d, r, v in zip(diag, res0, prod0)]
    res1 = [r - alpha0 * i for r, i in zip(res0, image0)]

    def matvec(vec_src, vec_tgt, columns):
        acol[...] = across(vec_src)
        half = NT // 2
        for h, acc in ((0, racc), (1, racc2)):
            spread = jnp.broadcast_to(vec_tgt[:, h * half:(h + 1) * half], (8, half))

            def step(r, sums):
                rows = pl.ds(pl.multiple_of(r * 8, 8), 8)
                p = plan[rows, h * half:(h + 1) * half]
                terms = p * spread
                parts = [terms[:, k * 128:(k + 1) * 128] for k in range(half // 128)]
                while len(parts) > 1:
                    parts = [parts[k] + parts[k + 1] for k in range(0, len(parts), 2)]
                acc[rows, :] = parts[0]
                if columns:
                    sums = sums + p * tiled(acol[rows, :], half // 128)
                return sums
            sums = lax.fori_loop(0, NS // 8, step, jnp.zeros((8, half), F32), unroll=2)
            if columns:
                col_b[0:1, h * half:(h + 1) * half] = jnp.sum(sums, axis=0, keepdims=True)
        return along(racc[...] + racc2[...])

    def scalars(res, row_part):
        norm = total(res[0] * res[0]) * (1.0 / TW) + total(res[2] * res[2]) * (1.0 / SW)
        quad = (
            total(res[0] * res[0] * diag[0]) * (1.0 / TW)
            + total(res[2] * res[2] * diag[2]) * (1.0 / SW)
            + 2.0 * total(res[0] * row_part)
        )
        return lanes(norm, quad)

    row_part = matvec(res1[0], res1[2], True)
    row_b[...] = row_part
    col_b[1:2, :] = tiled(scalars(res1, row_part), SW)

    push_all(SW, src_peer, lambda p: col_b.at[:, sub_of(p)], col_b_in.at[s], B_COL)
    push_all(TW, tgt_peer, lambda p: row_b, row_b_in.at[t], B_ROW)
    col_b_in[s] = col_b[:, my_sub]
    row_b_in[t] = row_b[...]
    wait_in(xg.at[pl.ds(0, 2), 0], G_RING3)
    before, after = lax.rem(z + ZS - 3, ZS), lax.rem(z + 3, ZS)
    top, rest = pl.ds(0, 16), pl.ds(16, 16)
    push(xg.at[before, core, top], xg.at[before, core, top], G_RING4, z_peer(1))
    push(xg.at[after, core, rest], xg.at[after, core, rest], G_RING4, z_peer(ZS - 1))
    vec_t[2:3, :] = res1[2]
    vec_s[:, 1, :] = res0[1]
    vec_s[:, 2, :] = res1[1]
    row_sums(2, 3)
    col_sums(0, 3, 0, 3)
    col_sums(0, 3, 6, 8)
    wait_in(xg.at[0, 0], G_RING4)
    for p in (3, ZS - 3, 4):
        zz = lax.rem(z + p, ZS)
        push(xg.at[zz, core], xg.at[zz, core], G_SIB2, sibling)

    wait_in(row_b_in.at[pl.ds(0, TW - 1)], B_ROW)
    row_full1 = jnp.sum(row_b_in[...], axis=0)
    agz_b[z] = row_full1
    wait_in(col_b_in.at[pl.ds(0, SW - 1)], B_COL)
    col_full1 = jnp.sum(col_b_in[...], axis=0)
    agc_b[:, my_sub] = col_full1[0:1, :]
    sc2_out[0] = col_full1[1:2, :]

    push_all(SW, src_peer, lambda p: agc_b.at[:, my_sub], agc_b.at[:, my_sub], B_AGC)
    push_all(TW, tgt_peer, lambda p: sc2_out.at[0], ags_b_in.at[t], B_AGS)
    push_all(ZS, z_peer, lambda p: agz_b.at[z], agz_b.at[z], B_AGZ)
    ags_b_in[t] = sc2_out[0]
    wait_in(xg.at[pl.ds(0, 3), 0], G_SIB2)
    lax.fori_loop(3, 6, q_block, 0)
    col_sums(0, 3, 3, 6)

    wait_in(agz_b.at[pl.ds(0, ZS - 1)], B_AGZ)
    wait_in(ags_b_in.at[pl.ds(0, TW - 1)], B_AGS)
    wait_in(agc_b.at[:, pl.ds(0, (SW - 1) * SUB)], B_AGC)
    sums = jnp.sum(ags_b_in[...], axis=0)
    norm1 = lane(sums, 0)
    beta0 = norm1 / norm0
    alpha1 = norm1 / (lane(sums, 1) - beta0 * norm1 / alpha0)
    prod1 = [row_full1, agz_b[:, 0, :], agc_b[...]]
    dir1 = [r1 + beta0 * r0 for r1, r0 in zip(res1, res0)]
    image1 = [d * r + v + beta0 * i for d, r, v, i in zip(diag, res1, prod1, image0)]
    res2 = [r - alpha1 * i for r, i in zip(res1, image1)]
    sol2 = [alpha0 * r0 + alpha1 * d1 for r0, d1 in zip(res0, dir1)]

    row_part = matvec(res2[0], res2[2], False)
    sc_out[...] = scalars(res2, row_part)

    push_all(SW, src_peer, lambda p: sc_out, sc_in.at[s], C_SRC)
    sc_in[s] = sc_out[...]

    vec_t[3:4, :] = res2[2]
    vec_s[:, 3, :] = res2[1]
    first_step = alpha0 + alpha1 * beta0

    def sums_of(points, out, v):
        low = v * STACK
        return points * out[low + 64:low + 65, :] - out[low:low + 64, :]

    def early_gradients(points, out, own, write):
        ones = sums_of(points, out, 0)
        zeroth = sums_of(points, out, 1)
        latest = sums_of(points, out, 2)
        write(0, (1.0 + first_step * own[0] + alpha1 * own[1]) * ones + first_step * zeroth + alpha1 * latest)
        write(1, (own[1] + beta0 * own[0]) * ones + latest + beta0 * zeroth)

    def late_gradient(points, out, own, write):
        write(2, own[2] * sums_of(points, out, 0) + sums_of(points, out, 3))

    def write_col(part, value):
        for k in range(XS):
            g_col[part, k] = value[k * 16:(k + 1) * 16, :]

    def write_row(part, value):
        for k in range(TW):
            g_row[part, k] = value[k * 8:(k + 1) * 8, :]

    early, late = pl.ds(0, 2), pl.ds(2, 1)
    own_t = vec_t[:, my_tile]
    own_t = [own_t[v:v + 1, :] for v in range(1, VECS)]
    own_s = [res0[0], res1[0], res2[0]]
    early_gradients(ysub[...], t_col, own_t, write_col)
    push_all(XS, x_peer, lambda p: g_col.at[early, lax.rem(x + p, XS)], g_col_in.at[x, early], D_COL)
    early_gradients(xs, t_row, own_s, write_row)
    push_all(TW, tgt_peer, lambda p: g_row.at[early, lax.rem(t + p, TW)], g_row_in.at[t, early], D_ROW)
    col_sums(3, 4)
    late_gradient(ysub[...], t_col, own_t, write_col)
    push_all(XS, x_peer, lambda p: g_col.at[late, lax.rem(x + p, XS)], g_col_in.at[x, late], D_COL2)
    g_col_in[x] = g_col[:, x]
    wait_in(sc_in.at[pl.ds(0, SW - 1)], C_SRC)
    sc2_out[1] = jnp.sum(sc_in[...], axis=0)
    push_all(TW, tgt_peer, lambda p: sc2_out.at[1], sc2_in.at[t], C_TGT)
    sc2_in[t] = sc2_out[1]

    row_sums(3, 4)
    late_gradient(xs, t_row, own_s, write_row)
    push_all(TW, tgt_peer, lambda p: g_row.at[late, lax.rem(t + p, TW)], g_row_in.at[t, late], D_ROW2)
    g_row_in[t] = g_row[:, t]

    wait_in(sc2_in.at[pl.ds(0, TW - 1)], C_TGT)
    sums = jnp.sum(sc2_in[...], axis=0)
    norm2 = lane(sums, 0)
    beta1 = norm2 / norm1
    alpha2 = norm2 / (lane(sums, 1) - beta1 * norm2 / alpha1)
    both = alpha2 * beta1

    def combine(parts):
        return (parts[0] + both * parts[1] + alpha2 * parts[2]) * (1.0 / EPSILON)

    def lead_of(zz):
        return pl.ds(pl.multiple_of(zz * TILE, TILE), LEAD)

    def rest_of(zz):
        return pl.ds(pl.multiple_of(zz * TILE + LEAD, 128), TILE - LEAD)

    wait_in(g_col_in.at[pl.ds(0, XS - 1), early], D_COL)
    wait_in(g_col_in.at[pl.ds(0, XS - 1), late], D_COL2)
    gt_ref[x, :, my_tile] = combine(jnp.sum(g_col_in[...], axis=0))
    mine = gt_ref.at[x, :, rest_of(z)]
    push_all(XS, x_peer, lambda p: mine, mine, O_XX)
    for p in (1, ZS - 1, 2, ZS - 2, 3, ZS - 3, 4):
        push(gt_ref.at[x, :, lead_of(z)], gt_ref.at[x, :, lead_of(z)], O_ZF, z_peer(p), IN_ZF + p)

    def lead_along_x(zz):
        for p in range(1, XS):
            push(gt_ref.at[x, :, lead_of(zz)], gt_ref.at[x, :, lead_of(zz)], O_ZF, x_peer(p), IN_XF + p)

    lead_along_x(z)

    sol_src_ref[...] = sol2[0] + both * dir1[0] + alpha2 * res2[0]
    sol_tgt_ref[...] = sol2[2] + both * dir1[2] + alpha2 * res2[2]

    wait_in(gt_ref.at[pl.ds(0, XS - 1), :, pl.ds(0, TILE - LEAD)], O_XX)
    push_all(
        ZS, z_peer, lambda p: gt_ref.at[:, :, rest_of(z)], gt_ref.at[:, :, rest_of(z)], O_XZ
    )
    for p in (1, ZS - 1, 2, ZS - 2, 3, ZS - 3, 4):
        zz = lax.rem(z + ZS - p, ZS)
        wait_in(gt_ref.at[x, :, lead_of(zz)], IN_ZF + p)
        lead_along_x(zz)
        if p == ZS - 1:
            wait_in(g_row_in.at[pl.ds(0, TW - 1), early], D_ROW)
            wait_in(g_row_in.at[pl.ds(0, TW - 1), late], D_ROW2)
            gs_ref[t] = combine(jnp.sum(g_row_in[...], axis=0))
            push_all(TW, tgt_peer, lambda p: gs_ref.at[t], gs_ref.at[t], O_ROW)

    wait_in(gs_ref.at[pl.ds(0, TW - 1)], O_ROW)
    wait_in(gt_ref.at[:, :, pl.ds(0, (ZS - 1) * (TILE - LEAD))], O_XZ)
    for p in range(1, XS):
        wait_in(gt_ref.at[0, :, pl.ds(0, ZS * LEAD)], IN_XF + p)

    wait_out(col_a_in.at[pl.ds(0, SW - 1)], A_COL)
    wait_out(row_a_in.at[pl.ds(0, TW - 1)], A_ROW)
    wait_out(init_in.at[pl.ds(0, ZS - 1)], A_INIT)
    wait_out(agc_a.at[:, pl.ds(0, (SW - 1) * SUB)], A_AGC)
    wait_out(agz_a.at[pl.ds(0, ZS - 1)], A_AGZ)
    wait_out(ags_a_in.at[pl.ds(0, TW - 1)], A_AGS)
    wait_out(col_b_in.at[pl.ds(0, SW - 1)], B_COL)
    wait_out(row_b_in.at[pl.ds(0, TW - 1)], B_ROW)
    wait_out(agc_b.at[:, pl.ds(0, (SW - 1) * SUB)], B_AGC)
    wait_out(agz_b.at[pl.ds(0, ZS - 1)], B_AGZ)
    wait_out(ags_b_in.at[pl.ds(0, TW - 1)], B_AGS)
    wait_out(sc_in.at[pl.ds(0, SW - 1)], C_SRC)
    wait_out(sc2_in.at[pl.ds(0, TW - 1)], C_TGT)
    wait_out(g_row_in.at[pl.ds(0, TW - 1), early], D_ROW)
    wait_out(g_col_in.at[pl.ds(0, XS - 1), early], D_COL)
    wait_out(g_row_in.at[pl.ds(0, TW - 1), late], D_ROW2)
    wait_out(g_col_in.at[pl.ds(0, XS - 1), late], D_COL2)
    wait_out(gs_ref.at[pl.ds(0, TW - 1)], O_ROW)
    wait_out(gt_ref.at[pl.ds(0, XS - 1), :, pl.ds(0, TILE - LEAD)], O_XX)
    wait_out(gt_ref.at[:, :, pl.ds(0, (ZS - 1) * (TILE - LEAD))], O_XZ)
    wait_out(gt_ref.at[pl.ds(0, 3), :, pl.ds(0, ZS * LEAD)], O_ZF)
    wait_out(gt_ref.at[0, :, pl.ds(0, (ZS - 1) * LEAD)], O_ZF)
    for k in (G_RING1, G_RING2, G_RING3):
        wait_out(xg.at[pl.ds(0, 2), 0], k)
    wait_out(xg.at[0, 0], G_RING4)
    wait_out(xg.at[pl.ds(0, 4), 0], G_SIB1)
    wait_out(xg.at[pl.ds(0, 3), 0], G_SIB2)


def hand_out(*refs):
    count = len(refs) // 2
    sems = refs[-1]
    copies = [pltpu.make_async_copy(refs[k], refs[count + k], sems.at[k]) for k in range(count)]
    for copy in copies:
        copy.start()
    for copy in copies:
        copy.wait()


def body(src_points, tgt_points, src_potential, tgt_potential, src_rhs, tgt_rhs):
    normalizer = 1.0 / math.sqrt(NS * SW * NT * TW)
    vmem = pl.BlockSpec(memory_space=pltpu.VMEM)
    far = pl.BlockSpec(memory_space=pltpu.HBM)

    def buf(*shape, dtype=F32):
        return pltpu.VMEM(shape, dtype)

    scratch = [
        buf(2, DIM // 2, NS), buf(DIM, NT), buf(1, NS), buf(1, NT), buf(1, NS), buf(1, NT),
        pltpu.SemaphoreType.DMA((6,)),
        buf(NS, NT), buf(NS, NT, dtype=BF16), buf(NS, NT, dtype=BF16),
        buf(ZS, NS, TILE, dtype=BF16), buf(ZS, NS, TILE, dtype=BF16),
        buf(NS, 256, dtype=BF16), buf(256, NT, dtype=BF16),
        buf(NS, 128), buf(NS, 128), buf(NS, 128), buf(NS, 128),
        buf(4, NT), buf(SW, 4, SUB), buf(2, NS), buf(TW, 2, NS),
        buf(2, NS), buf(ZS, 2, NS),
        buf(2, NT), buf(ZS, 2, NS), buf(1, 128), buf(TW, 1, 128),
        buf(2, NT), buf(SW, 2, SUB), buf(1, NS), buf(TW, 1, NS),
        buf(1, NT), buf(ZS, 1, NS), buf(TW, 1, 128),
        buf(1, 128), buf(SW, 1, 128), buf(2, 1, 128), buf(TW, 1, 128),
        buf(DIM, TILE), buf(VECS, NT), buf(ZS, VECS, NS),
        buf(2 * 3 * STACK, TILE, dtype=BF16),
        buf(VECS * STACK, NS), buf(VECS * STACK, TILE),
        buf(3, TW, 8, NS), buf(TW, 3, 8, NS),
        buf(3, XS, 16, TILE), buf(XS, 3, 16, TILE),
        buf(ZS, 2, DIM // 2, NS),
        pltpu.SemaphoreType.DMA((N_SEMS,)), pltpu.SemaphoreType.DMA((N_IN,)),
    ]
    shapes = (
        jax.ShapeDtypeStruct((1, NS), F32),
        jax.ShapeDtypeStruct((1, NT), F32),
        jax.ShapeDtypeStruct((TW, 8, NS), F32),
        jax.ShapeDtypeStruct((XS, 16, NT), F32),
    )
    results = pl.pallas_call(
        functools.partial(kernel, math.log2(normalizer)),
        out_shape=shapes,
        in_specs=[far] * 6,
        out_specs=[vmem] * 4,
        scratch_shapes=scratch,
        compiler_params=pltpu.CompilerParams(
            collective_id=1, has_side_effects=True, vmem_limit_bytes=60 * 1024 * 1024
        ),
    )(
        src_points.reshape(2, DIM // 2, NS), tgt_points, src_potential.reshape(1, NS),
        tgt_potential.reshape(1, NT), src_rhs.reshape(1, NS), tgt_rhs.reshape(1, NT),
    )
    sol_src, sol_tgt, grad_src, grad_tgt = pl.pallas_call(
        hand_out,
        out_shape=shapes,
        in_specs=[vmem] * 4,
        out_specs=[far] * 4,
        scratch_shapes=[pltpu.SemaphoreType.DMA((4,))],
    )(*results)
    return (
        sol_src.reshape(NS), sol_tgt.reshape(NT), grad_src.reshape(DIM, NS), grad_tgt.reshape(DIM, NT)
    )


def solution(mesh):
    return jax.shard_map(
        body,
        mesh=mesh,
        in_specs=(P(None, "src"), P(None, "tgt"), P("src"), P("tgt"), P("src"), P("tgt")),
        out_specs=(P("src"), P("tgt"), P(None, "src"), P(None, "tgt")),
        check_vma=False,
    )
```

```python
import functools
import math

import jax
import jax.numpy as jnp
from jax import lax
from jax.experimental import pallas as pl
from jax.experimental.pallas import tpu as pltpu
from jax.sharding import PartitionSpec as P

EPSILON = 0.5
REGULARIZER = 1.0
LOG2E = math.log2(math.e)
MESH = pl.DeviceIdType.MESH
F32 = jnp.float32
BF16 = jnp.bfloat16

XS, ZS = 4, 8
SW, TW = XS * ZS, 8
DIM = 64
NS, NT = 512, 4096
SUB = NT // SW
TILE = 512
STEP = 128
ROWS = 64
STACK = 80
VECS = 4

(A_COL, A_ROW, A_INIT, A_AGC, A_AGZ, A_AGS, B_COL, B_ROW, B_AGC, B_AGZ, B_AGS, C_SRC, C_TGT,
 D_ROW, D_COL, D_ROW2, D_COL2, O_ROW, O_XX, O_XZ, O_ZF, G_NEAR, G_FAR, G_SIB1, G_SIB2) = range(25)
IN_ZF = 25
IN_XF = IN_ZF + ZS
N_SEMS = 25
N_IN = IN_XF + XS
LEAD = 384


def halves(value):
    high = value.astype(BF16)
    return high, (value - high.astype(F32)).astype(BF16)


def across(vector):
    return jnp.broadcast_to(vector, (128, vector.shape[1])).T


def along(block):
    return jnp.sum(block.T, axis=0, keepdims=True)


def tiled(block, times):
    return jnp.concatenate([block] * times, axis=1)


def lane_tiles(value):
    parts = [value[:, k:k + 128] for k in range(0, value.shape[1], 128)]
    while len(parts) > 1:
        parts = [parts[k] + parts[k + 1] for k in range(0, len(parts), 2)]
    return parts[0]


def fold(vector):
    return lane_tiles(vector)


def across_lanes(rows):
    return jnp.sum(rows, axis=1, keepdims=True)


def kernel(
    shift, xs_hbm, yt_hbm, f_hbm, g_hbm, a0_hbm, b0_hbm,
    sol_src_ref, sol_tgt_ref, gs_ref, gt_ref,
    xs_ref, yt_ref, f_ref, g_ref, a0_ref, b0_ref, load,
    plan, plan_hi, plan_lo, q_hi, q_lo, x4t, y4, fcol, acol, racc, racc2,
    col_a, col_a_in, row_a, row_a_in, init_out, init_in, agc_a, agz_a, ags_a, ags_a_in,
    col_b, col_b_in, row_b, row_b_in, agc_b, agz_b, ags_b_in,
    sc_out, sc_in, sc2_out, sc2_in, ysub, vec_t, vec_s, stack, t_row, t_col,
    g_row, g_row_in, g_col, g_col_in, xg, send, recv,
):
    loads = [
        pltpu.make_async_copy(far, near, load.at[k])
        for k, (far, near) in enumerate((
            (yt_hbm, yt_ref), (xs_hbm, xs_ref), (f_hbm, f_ref), (g_hbm, g_ref), (a0_hbm, a0_ref), (b0_hbm, b0_ref),
        ))
    ]
    for copy in loads:
        copy.start()
    s = lax.axis_index("src")
    t = lax.axis_index("tgt")
    x, z = s // ZS, s % ZS
    core = t % 2
    sibling = (s, t + 1 - 2 * core)

    def src_peer(p):
        return (lax.rem(s + p, SW), t)

    def tgt_peer(p):
        return (s, lax.rem(t + p, TW))

    def z_peer(p):
        return (x * ZS + lax.rem(z + p, ZS), t)

    def x_peer(p):
        return (lax.rem(x + p, XS) * ZS + z, t)

    def push(src, dst, k, device, k_recv=None):
        pltpu.make_async_remote_copy(
            src_ref=src, dst_ref=dst, send_sem=send.at[k],
            recv_sem=recv.at[k if k_recv is None else k_recv],
            device_id=device, device_id_type=MESH,
        ).start()

    def push_all(ways, peer, src, dst, k):
        def step(p, carry):
            push(src(p), dst, k, peer(p))
            return carry
        lax.fori_loop(1, ways, step, 0)

    def wait_in(ref, k):
        pltpu.make_async_copy(ref, ref, recv.at[k]).wait()

    def wait_out(ref, k):
        pltpu.make_async_copy(ref, ref, send.at[k]).wait()

    def sub_of(p):
        return pl.ds(pl.multiple_of(lax.rem(s + p, SW) * SUB, SUB), SUB)

    my_sub = pl.ds(pl.multiple_of(s * SUB, SUB), SUB)
    my_tile = pl.ds(pl.multiple_of(z * TILE, TILE), TILE)

    barrier = pltpu.get_barrier_semaphore()

    def greet(ways, peer):
        def step(p, carry):
            pl.semaphore_signal(barrier, inc=1, device_id=peer(p), device_id_type=MESH)
            return carry
        lax.fori_loop(1, ways, step, 0)

    greet(SW, src_peer)
    greet(TW, tgt_peer)
    for copy in loads[1:]:
        copy.wait()

    xs = jnp.concatenate([xs_ref[0], xs_ref[1]], axis=0)
    a0 = a0_ref[...]
    b0 = b0_ref[...]

    def x_parts(points):
        scaled = points * (LOG2E / EPSILON)
        high = scaled.astype(BF16).astype(F32)
        low = scaled - high
        return jnp.concatenate([high, high, low, low], axis=0).T.astype(BF16)

    x4t[...] = x_parts(xs)

    fcol[...] = across(f_ref[...] * LOG2E + shift)
    acol[...] = across(a0)
    racc[...] = jnp.zeros_like(racc)
    racc2[...] = jnp.zeros_like(racc2)

    loads[0].wait()

    def plan_step(n, carry):
        cs = pl.ds(pl.multiple_of(n * STEP, STEP), STEP)
        high, low = halves(yt_ref[:, cs])
        parts = jnp.concatenate([high, low, high, low], axis=0)
        y4[:, cs] = parts
        cross = jnp.dot(x4t[...], parts, preferred_element_type=F32)
        g_now = g_ref[:, cs] * LOG2E
        b_now = b0_ref[:, cs]
        mass_sum = jnp.zeros((8, STEP), F32)
        a_sum = jnp.zeros((8, STEP), F32)
        for r in range(0, NS, ROWS):
            p = jnp.exp2(cross[r:r + ROWS, :] + tiled(fcol[r:r + ROWS, :], STEP // 128) + g_now)
            plan[r:r + ROWS, cs] = p
            racc[r:r + ROWS, :] += lane_tiles(p)
            racc2[r:r + ROWS, :] += lane_tiles(p * b_now)
            pa = p * tiled(acol[r:r + ROWS, :], STEP // 128)
            mass_sum = mass_sum + jnp.sum(p.reshape(ROWS // 8, 8, STEP), axis=0)
            a_sum = a_sum + jnp.sum(pa.reshape(ROWS // 8, 8, STEP), axis=0)
        col_a[0:1, cs] = jnp.sum(mass_sum, axis=0, keepdims=True)
        col_a[1:2, cs] = jnp.sum(a_sum, axis=0, keepdims=True)
        return carry
    lax.fori_loop(0, NT // STEP, plan_step, 0, unroll=2)

    mass_part = along(racc[...])
    v_part = along(racc2[...])
    row_a[0:1, :] = mass_part
    row_a[1:2, :] = v_part
    init_out[0:1, :] = f_ref[...]
    init_out[1:2, :] = a0
    norm_part = fold(a0 * a0) * (1.0 / TW) + fold(b0 * b0) * (1.0 / SW)
    quad_part = (
        norm_part * REGULARIZER + fold(a0 * (a0 * mass_part + 2.0 * v_part))
        + fold(b0 * b0 * col_a[0:1, :])
    )
    col_a[2:3, :] = tiled(norm_part, SW)
    col_a[3:4, :] = tiled(quad_part, SW)

    pl.semaphore_wait(barrier, SW - 1 + TW - 1)

    push_all(SW, src_peer, lambda p: col_a.at[:, sub_of(p)], col_a_in.at[s], A_COL)
    push_all(TW, tgt_peer, lambda p: row_a, row_a_in.at[t], A_ROW)
    push_all(ZS, z_peer, lambda p: init_out, init_in.at[z], A_INIT)
    for p in (1, ZS - 1, 2, ZS - 2):
        push(xs_ref.at[core], xg.at[z, core], G_NEAR, z_peer(p))
    col_a_in[s] = col_a[:, my_sub]
    row_a_in[t] = row_a[...]
    init_in[z] = init_out[...]
    xg[z, 0] = xs_ref[0]
    xg[z, 1] = xs_ref[1]
    ysub[...] = yt_ref[:, my_tile]

    g_sub = g_ref[:, my_tile] * LOG2E

    def q_block(p, carry):
        zz = lax.rem(z + p, ZS)
        points = jnp.concatenate([xg[zz, 0], xg[zz, 1]], axis=0)
        fcol[...] = across(init_in[zz][0:1, :] * LOG2E + shift)
        parts = x_parts(points)
        for c in range(0, TILE, 128):
            some = pl.ds(pl.multiple_of(z * TILE + c, 128), 128)
            cross = jnp.dot(parts, y4[:, some], preferred_element_type=F32)
            for r in range(0, NS, 64):
                value = jnp.exp2(cross[r:r + 64, :] + fcol[r:r + 64, :] + g_sub[:, c:c + 128])
                high, low = halves(value)
                q_hi[zz, r:r + 64, c:c + 128] = high
                q_lo[zz, r:r + 64, c:c + 128] = low
        return carry

    def fill_stack(points, weights):
        count = len(weights)
        for v, weight in enumerate(weights):
            value = jnp.concatenate([points * weight, jnp.broadcast_to(weight, (16, TILE))], axis=0)
            high, low = halves(value)
            stack[v * STACK:(v + 1) * STACK, :] = high
            stack[(count + v) * STACK:(count + v + 1) * STACK, :] = low

    def add_sums(out, low, count, plan_high, plan_low, dims):
        rows = count * STACK
        first = lax.dot_general(
            stack[0:2 * rows, :], plan_high, (dims, ((), ())), preferred_element_type=F32
        )
        second = lax.dot_general(
            stack[0:rows, :], plan_low, (dims, ((), ())), preferred_element_type=F32
        )
        out[low * STACK:low * STACK + rows, :] += first[0:rows, :] + first[rows:, :] + second

    def row_sums(low, high, split=False):
        def step(n, carry):
            cs = pl.ds(pl.multiple_of(n * TILE, TILE), TILE)
            if split:
                for r in range(0, NS, 64):
                    top, rest = halves(plan[r:r + 64, cs])
                    plan_hi[r:r + 64, cs] = top
                    plan_lo[r:r + 64, cs] = rest
            fill_stack(yt_ref[:, cs], [vec_t[v:v + 1, cs] for v in range(low, high)])
            add_sums(t_row, low, high - low, plan_hi[:, cs], plan_lo[:, cs], ((1,), (1,)))
            return carry
        lax.fori_loop(0, NT // TILE, step, 0)

    def col_sums(low, high, first=0, last=ZS):
        def step(p, carry):
            zz = lax.rem(z + p, ZS)
            fill_stack(
                jnp.concatenate([xg[zz, 0], xg[zz, 1]], axis=0),
                [vec_s[zz, v:v + 1, :] for v in range(low, high)],
            )
            add_sums(t_col, low, high - low, q_hi[zz], q_lo[zz], ((1,), (0,)))
            return carry
        lax.fori_loop(first, last, step, 0)

    t_row[...] = jnp.zeros_like(t_row)
    t_col[...] = jnp.zeros_like(t_col)
    vec_t[0:1, :] = jnp.ones((1, NT), F32)
    vec_t[1:2, :] = b0
    vec_s[:, 0, :] = jnp.ones((ZS, NS), F32)
    row_sums(0, 2, split=True)

    wait_in(row_a_in.at[pl.ds(0, TW - 1)], A_ROW)
    row_full = jnp.sum(row_a_in[...], axis=0)
    agz_own = row_full
    wait_in(col_a_in.at[pl.ds(0, SW - 1)], A_COL)
    col_full = jnp.sum(col_a_in[...], axis=0)
    agc_a[:, my_sub] = col_full[0:2, :]
    ags_a[...] = col_full[2:4, :]
    agz_a[z] = agz_own

    push_all(SW, src_peer, lambda p: agc_a.at[:, my_sub], agc_a.at[:, my_sub], A_AGC)
    push_all(TW, tgt_peer, lambda p: ags_a, ags_a_in.at[t], A_AGS)
    push_all(ZS, z_peer, lambda p: agz_a.at[z], agz_a.at[z], A_AGZ)
    ags_a_in[t] = ags_a[...]
    wait_in(init_in.at[pl.ds(0, ZS - 1)], A_INIT)
    wait_in(xg.at[pl.ds(0, 4), 0], G_NEAR)
    before, after = lax.rem(z + ZS - 2, ZS), lax.rem(z + 2, ZS)
    top, rest = pl.ds(0, 16), pl.ds(16, 16)
    push(xg.at[before, core], xg.at[before, core], G_FAR, z_peer(1))
    push(xg.at[after, core], xg.at[after, core], G_FAR, z_peer(ZS - 1))
    push(xg.at[before, core, top], xg.at[before, core, top], G_FAR, z_peer(2))
    push(xg.at[after, core, rest], xg.at[after, core, rest], G_FAR, z_peer(ZS - 2))
    for p in (1, ZS - 1, 2, ZS - 2):
        zz = lax.rem(z + p, ZS)
        push(xg.at[zz, core], xg.at[zz, core], G_SIB1, sibling)
    q_block(0, 0)
    wait_in(xg.at[pl.ds(0, 4), 0], G_SIB1)
    lax.fori_loop(1, 3, q_block, 0)
    lax.fori_loop(6, 8, q_block, 0)

    wait_in(agz_a.at[pl.ds(0, ZS - 1)], A_AGZ)
    wait_in(ags_a_in.at[pl.ds(0, TW - 1)], A_AGS)
    wait_in(agc_a.at[:, pl.ds(0, (SW - 1) * SUB)], A_AGC)
    sums = jnp.sum(ags_a_in[...], axis=0)
    norm0 = across_lanes(sums[0:1, :])
    alpha0 = norm0 / across_lanes(sums[1:2, :])

    diag = [row_full[0:1, :] + REGULARIZER, agz_a[:, 0, :] + REGULARIZER, agc_a[0:1, :] + REGULARIZER]
    res0 = [a0, init_in[:, 1, :], b0]
    prod0 = [row_full[1:2, :], agz_a[:, 1, :], agc_a[1:2, :]]
    image0 = [d * r + v for d, r, v in zip(diag, res0, prod0)]
    res1 = [r - alpha0 * i for r, i in zip(res0, image0)]

    def matvec(vec_src, vec_tgt, columns):
        acol[...] = across(vec_src)
        half = NT // 2
        for h, acc in ((0, racc), (1, racc2)):
            spread = jnp.broadcast_to(vec_tgt[:, h * half:(h + 1) * half], (8, half))

            def step(r, sums):
                rows = pl.ds(pl.multiple_of(r * 8, 8), 8)
                p = plan[rows, h * half:(h + 1) * half]
                terms = p * spread
                parts = [terms[:, k * 128:(k + 1) * 128] for k in range(half // 128)]
                while len(parts) > 1:
                    parts = [parts[k] + parts[k + 1] for k in range(0, len(parts), 2)]
                acc[rows, :] = parts[0]
                if columns:
                    sums = sums + p * tiled(acol[rows, :], half // 128)
                return sums
            sums = lax.fori_loop(0, NS // 8, step, jnp.zeros((8, half), F32), unroll=2)
            if columns:
                col_b[0:1, h * half:(h + 1) * half] = jnp.sum(sums, axis=0, keepdims=True)
        return along(racc[...] + racc2[...])

    def scalars(res, row_part):
        norm = fold(res[0] * res[0]) * (1.0 / TW) + fold(res[2] * res[2]) * (1.0 / SW)
        quad = (
            fold(res[0] * (res[0] * diag[0] * (1.0 / TW) + 2.0 * row_part))
            + fold(res[2] * res[2] * diag[2]) * (1.0 / SW)
        )
        return norm, quad

    row_part = matvec(res1[0], res1[2], True)
    row_b[...] = row_part
    norm_part, quad_part = scalars(res1, row_part)
    col_b[1:2, :] = tiled(norm_part, SW)
    col_b[2:3, :] = tiled(quad_part, SW)
    col_b[3:4, :] = jnp.zeros((1, NT), F32)

    push_all(SW, src_peer, lambda p: col_b.at[:, sub_of(p)], col_b_in.at[s], B_COL)
    push_all(TW, tgt_peer, lambda p: row_b, row_b_in.at[t], B_ROW)
    col_b_in[s] = col_b[:, my_sub]
    row_b_in[t] = row_b[...]
    vec_t[2:3, :] = res1[2]
    vec_s[:, 1, :] = res0[1]
    vec_s[:, 2, :] = res1[1]
    row_sums(2, 3)
    wait_in(xg.at[pl.ds(0, 3), 0], G_FAR)
    for p in (3, ZS - 3, 4):
        zz = lax.rem(z + p, ZS)
        push(xg.at[zz, core], xg.at[zz, core], G_SIB2, sibling)
    col_sums(0, 3, 0, 3)
    col_sums(0, 3, 6, 8)

    wait_in(row_b_in.at[pl.ds(0, TW - 1)], B_ROW)
    row_full1 = jnp.sum(row_b_in[...], axis=0)
    agz_b[z] = row_full1
    wait_in(col_b_in.at[pl.ds(0, SW - 1)], B_COL)
    col_full1 = jnp.sum(col_b_in[...], axis=0)
    agc_b[:, my_sub] = col_full1[0:1, :]
    sc2_out[0] = col_full1[1:3, :]

    push_all(SW, src_peer, lambda p: agc_b.at[:, my_sub], agc_b.at[:, my_sub], B_AGC)
    push_all(TW, tgt_peer, lambda p: sc2_out.at[0], ags_b_in.at[t], B_AGS)
    push_all(ZS, z_peer, lambda p: agz_b.at[z], agz_b.at[z], B_AGZ)
    ags_b_in[t] = sc2_out[0]
    wait_in(xg.at[pl.ds(0, 3), 0], G_SIB2)
    lax.fori_loop(3, 6, q_block, 0)
    col_sums(0, 3, 3, 6)

    wait_in(agz_b.at[pl.ds(0, ZS - 1)], B_AGZ)
    wait_in(ags_b_in.at[pl.ds(0, TW - 1)], B_AGS)
    wait_in(agc_b.at[:, pl.ds(0, (SW - 1) * SUB)], B_AGC)
    sums = jnp.sum(ags_b_in[...], axis=0)
    norm1 = across_lanes(sums[0:1, :])
    beta0 = norm1 / norm0
    alpha1 = norm1 / (across_lanes(sums[1:2, :]) - beta0 * norm1 / alpha0)
    prod1 = [row_full1, agz_b[:, 0, :], agc_b[...]]
    dir1 = [r1 + beta0 * r0 for r1, r0 in zip(res1, res0)]
    image1 = [d * r + v + beta0 * i for d, r, v, i in zip(diag, res1, prod1, image0)]
    res2 = [r - alpha1 * i for r, i in zip(res1, image1)]
    sol2 = [alpha0 * r0 + alpha1 * d1 for r0, d1 in zip(res0, dir1)]

    row_part = matvec(res2[0], res2[2], False)
    norm_part, quad_part = scalars(res2, row_part)
    sc_out[0:1, :] = norm_part
    sc_out[1:2, :] = quad_part

    push_all(SW, src_peer, lambda p: sc_out, sc_in.at[s], C_SRC)
    sc_in[s] = sc_out[...]

    vec_t[3:4, :] = res2[2]
    vec_s[:, 3, :] = res2[1]
    first_step = alpha0 + alpha1 * beta0

    def sums_of(points, out, v):
        low = v * STACK
        return points * out[low + 64:low + 65, :] - out[low:low + 64, :]

    def early_gradients(points, out, own, write):
        ones = sums_of(points, out, 0)
        zeroth = sums_of(points, out, 1)
        latest = sums_of(points, out, 2)
        write(0, (1.0 + first_step * own[0] + alpha1 * own[1]) * ones + first_step * zeroth + alpha1 * latest)
        write(1, (own[1] + beta0 * own[0]) * ones + latest + beta0 * zeroth)

    def late_gradient(points, out, own, write):
        write(2, own[2] * sums_of(points, out, 0) + sums_of(points, out, 3))

    def write_col(part, value):
        for k in range(XS):
            g_col[part, k] = value[k * 16:(k + 1) * 16, :]

    def write_row(part, value):
        for k in range(TW):
            g_row[part, k] = value[k * 8:(k + 1) * 8, :]

    early, late = pl.ds(0, 2), pl.ds(2, 1)
    own_t = vec_t[:, my_tile]
    own_t = [own_t[v:v + 1, :] for v in range(1, VECS)]
    own_s = [res0[0], res1[0], res2[0]]
    early_gradients(ysub[...], t_col, own_t, write_col)
    push_all(XS, x_peer, lambda p: g_col.at[early, lax.rem(x + p, XS)], g_col_in.at[x, early], D_COL)
    early_gradients(xs, t_row, own_s, write_row)
    push_all(TW, tgt_peer, lambda p: g_row.at[early, lax.rem(t + p, TW)], g_row_in.at[t, early], D_ROW)
    col_sums(3, 4)
    late_gradient(ysub[...], t_col, own_t, write_col)
    push_all(XS, x_peer, lambda p: g_col.at[late, lax.rem(x + p, XS)], g_col_in.at[x, late], D_COL2)
    g_col_in[x] = g_col[:, x]
    wait_in(sc_in.at[pl.ds(0, SW - 1)], C_SRC)
    sc2_out[1] = jnp.sum(sc_in[...], axis=0)
    push_all(TW, tgt_peer, lambda p: sc2_out.at[1], sc2_in.at[t], C_TGT)
    sc2_in[t] = sc2_out[1]

    row_sums(3, 4)
    late_gradient(xs, t_row, own_s, write_row)
    push_all(TW, tgt_peer, lambda p: g_row.at[late, lax.rem(t + p, TW)], g_row_in.at[t, late], D_ROW2)
    g_row_in[t] = g_row[:, t]

    wait_in(sc2_in.at[pl.ds(0, TW - 1)], C_TGT)
    sums = jnp.sum(sc2_in[...], axis=0)
    norm2 = across_lanes(sums[0:1, :])
    beta1 = norm2 / norm1
    alpha2 = norm2 / (across_lanes(sums[1:2, :]) - beta1 * norm2 / alpha1)
    both = alpha2 * beta1

    def combine(parts):
        return (parts[0] + both * parts[1] + alpha2 * parts[2]) * (1.0 / EPSILON)

    def lead_of(zz):
        return pl.ds(pl.multiple_of(zz * TILE, TILE), LEAD)

    def rest_of(zz):
        return pl.ds(pl.multiple_of(zz * TILE + LEAD, 128), TILE - LEAD)

    wait_in(g_col_in.at[pl.ds(0, XS - 1), early], D_COL)
    wait_in(g_col_in.at[pl.ds(0, XS - 1), late], D_COL2)
    gt_ref[x, :, my_tile] = combine(jnp.sum(g_col_in[...], axis=0))
    mine = gt_ref.at[x, :, rest_of(z)]
    push_all(XS, x_peer, lambda p: mine, mine, O_XX)
    for p in (1, ZS - 1, 2, ZS - 2, 3, ZS - 3, 4):
        push(gt_ref.at[x, :, lead_of(z)], gt_ref.at[x, :, lead_of(z)], O_ZF, z_peer(p), IN_ZF + p)

    def lead_along_x(zz):
        for p in range(1, XS):
            push(gt_ref.at[x, :, lead_of(zz)], gt_ref.at[x, :, lead_of(zz)], O_ZF, x_peer(p), IN_XF + p)

    lead_along_x(z)

    sol_src_ref[...] = sol2[0] + both * dir1[0] + alpha2 * res2[0]
    sol_tgt_ref[...] = sol2[2] + both * dir1[2] + alpha2 * res2[2]

    wait_in(gt_ref.at[pl.ds(0, XS - 1), :, pl.ds(0, TILE - LEAD)], O_XX)
    push_all(
        ZS, z_peer, lambda p: gt_ref.at[:, :, rest_of(z)], gt_ref.at[:, :, rest_of(z)], O_XZ
    )
    for p in (1, ZS - 1, 2, ZS - 2, 3, ZS - 3, 4):
        zz = lax.rem(z + ZS - p, ZS)
        wait_in(gt_ref.at[x, :, lead_of(zz)], IN_ZF + p)
        lead_along_x(zz)
        if p == ZS - 1:
            wait_in(g_row_in.at[pl.ds(0, TW - 1), early], D_ROW)
            wait_in(g_row_in.at[pl.ds(0, TW - 1), late], D_ROW2)
            gs_ref[t] = combine(jnp.sum(g_row_in[...], axis=0))
            push_all(TW, tgt_peer, lambda p: gs_ref.at[t], gs_ref.at[t], O_ROW)

    wait_in(gs_ref.at[pl.ds(0, TW - 1)], O_ROW)
    wait_in(gt_ref.at[:, :, pl.ds(0, (ZS - 1) * (TILE - LEAD))], O_XZ)
    for p in range(1, XS):
        wait_in(gt_ref.at[0, :, pl.ds(0, ZS * LEAD)], IN_XF + p)

    wait_out(col_a_in.at[pl.ds(0, SW - 1)], A_COL)
    wait_out(row_a_in.at[pl.ds(0, TW - 1)], A_ROW)
    wait_out(init_in.at[pl.ds(0, ZS - 1)], A_INIT)
    wait_out(agc_a.at[:, pl.ds(0, (SW - 1) * SUB)], A_AGC)
    wait_out(agz_a.at[pl.ds(0, ZS - 1)], A_AGZ)
    wait_out(ags_a_in.at[pl.ds(0, TW - 1)], A_AGS)
    wait_out(col_b_in.at[pl.ds(0, SW - 1)], B_COL)
    wait_out(row_b_in.at[pl.ds(0, TW - 1)], B_ROW)
    wait_out(agc_b.at[:, pl.ds(0, (SW - 1) * SUB)], B_AGC)
    wait_out(agz_b.at[pl.ds(0, ZS - 1)], B_AGZ)
    wait_out(ags_b_in.at[pl.ds(0, TW - 1)], B_AGS)
    wait_out(sc_in.at[pl.ds(0, SW - 1)], C_SRC)
    wait_out(sc2_in.at[pl.ds(0, TW - 1)], C_TGT)
    wait_out(g_row_in.at[pl.ds(0, TW - 1), early], D_ROW)
    wait_out(g_col_in.at[pl.ds(0, XS - 1), early], D_COL)
    wait_out(g_row_in.at[pl.ds(0, TW - 1), late], D_ROW2)
    wait_out(g_col_in.at[pl.ds(0, XS - 1), late], D_COL2)
    wait_out(gs_ref.at[pl.ds(0, TW - 1)], O_ROW)
    wait_out(gt_ref.at[pl.ds(0, XS - 1), :, pl.ds(0, TILE - LEAD)], O_XX)
    wait_out(gt_ref.at[:, :, pl.ds(0, (ZS - 1) * (TILE - LEAD))], O_XZ)
    wait_out(gt_ref.at[pl.ds(0, 3), :, pl.ds(0, ZS * LEAD)], O_ZF)
    wait_out(gt_ref.at[0, :, pl.ds(0, (ZS - 1) * LEAD)], O_ZF)
    wait_out(xg.at[pl.ds(0, 4), 0], G_NEAR)
    wait_out(xg.at[pl.ds(0, 3), 0], G_FAR)
    wait_out(xg.at[pl.ds(0, 4), 0], G_SIB1)
    wait_out(xg.at[pl.ds(0, 3), 0], G_SIB2)


def hand_out(*refs):
    sems = refs[-1]
    parts = [(refs[3].at[k], refs[7].at[k], refs[11].at[k]) for k in range(XS)]
    parts += [(refs[k], refs[4 + k], refs[8 + k]) for k in (2, 1, 0)]
    loads = [pltpu.make_async_copy(src, near, sems.at[k]) for k, (src, _, near) in enumerate(parts)]
    stores = [
        pltpu.make_async_copy(near, dst, sems.at[len(parts) + k])
        for k, (_, dst, near) in enumerate(parts)
    ]
    for load in loads:
        load.start()
    for load, store in zip(loads, stores):
        load.wait()
        store.start()
    for store in stores:
        store.wait()


def body(src_points, tgt_points, src_potential, tgt_potential, src_rhs, tgt_rhs):
    normalizer = 1.0 / math.sqrt(NS * SW * NT * TW)
    vmem = pl.BlockSpec(memory_space=pltpu.VMEM)
    far = pl.BlockSpec(memory_space=pltpu.HBM)

    def buf(*shape, dtype=F32):
        return pltpu.VMEM(shape, dtype)

    scratch = [
        buf(2, DIM // 2, NS), buf(DIM, NT), buf(1, NS), buf(1, NT), buf(1, NS), buf(1, NT),
        pltpu.SemaphoreType.DMA((6,)),
        buf(NS, NT), buf(NS, NT, dtype=BF16), buf(NS, NT, dtype=BF16),
        buf(ZS, NS, TILE, dtype=BF16), buf(ZS, NS, TILE, dtype=BF16),
        buf(NS, 256, dtype=BF16), buf(256, NT, dtype=BF16),
        buf(NS, 128), buf(NS, 128), buf(NS, 128), buf(NS, 128),
        buf(4, NT), buf(SW, 4, SUB), buf(2, NS), buf(TW, 2, NS),
        buf(2, NS), buf(ZS, 2, NS),
        buf(2, NT), buf(ZS, 2, NS), buf(2, 128), buf(TW, 2, 128),
        buf(4, NT), buf(SW, 4, SUB), buf(1, NS), buf(TW, 1, NS),
        buf(1, NT), buf(ZS, 1, NS), buf(TW, 2, 128),
        buf(2, 128), buf(SW, 2, 128), buf(2, 2, 128), buf(TW, 2, 128),
        buf(DIM, TILE), buf(VECS, NT), buf(ZS, VECS, NS),
        buf(2 * 3 * STACK, TILE, dtype=BF16),
        buf(VECS * STACK, NS), buf(VECS * STACK, TILE),
        buf(3, TW, 8, NS), buf(TW, 3, 8, NS),
        buf(3, XS, 16, TILE), buf(XS, 3, 16, TILE),
        buf(ZS, 2, DIM // 2, NS),
        pltpu.SemaphoreType.DMA((N_SEMS,)), pltpu.SemaphoreType.DMA((N_IN,)),
    ]
    shapes = (
        jax.ShapeDtypeStruct((1, NS), F32),
        jax.ShapeDtypeStruct((1, NT), F32),
        jax.ShapeDtypeStruct((TW, 8, NS), F32),
        jax.ShapeDtypeStruct((XS, 16, NT), F32),
    )
    results = pl.pallas_call(
        functools.partial(kernel, math.log2(normalizer)),
        out_shape=shapes,
        in_specs=[far] * 6,
        out_specs=[vmem] * 4,
        scratch_shapes=scratch,
        compiler_params=pltpu.CompilerParams(
            collective_id=1, has_side_effects=True, vmem_limit_bytes=60 * 1024 * 1024
        ),
    )(
        src_points.reshape(2, DIM // 2, NS), tgt_points, src_potential.reshape(1, NS),
        tgt_potential.reshape(1, NT), src_rhs.reshape(1, NS), tgt_rhs.reshape(1, NT),
    )
    sol_src, sol_tgt, grad_src, grad_tgt = pl.pallas_call(
        hand_out,
        out_shape=shapes,
        in_specs=[far] * 4,
        out_specs=[far] * 4,
        scratch_shapes=[buf(*shape.shape) for shape in shapes] + [pltpu.SemaphoreType.DMA((2 * (XS + 3),))],
        compiler_params=pltpu.CompilerParams(vmem_limit_bytes=60 * 1024 * 1024),
    )(*results)
    return (
        sol_src.reshape(NS), sol_tgt.reshape(NT), grad_src.reshape(DIM, NS), grad_tgt.reshape(DIM, NT)
    )


def solution(mesh):
    return jax.shard_map(
        body,
        mesh=mesh,
        in_specs=(P(None, "src"), P(None, "tgt"), P("src"), P("tgt"), P("src"), P("tgt")),
        out_specs=(P("src"), P("tgt"), P(None, "src"), P(None, "tgt")),
        check_vma=False,
    )
```

```python
import functools
import math

import jax
import jax.numpy as jnp
from jax import lax
from jax.experimental import pallas as pl
from jax.experimental.pallas import tpu as pltpu
from jax.sharding import PartitionSpec as P

EPSILON = 0.5
REGULARIZER = 1.0
LOG2E = math.log2(math.e)
MESH = pl.DeviceIdType.MESH
F32 = jnp.float32
BF16 = jnp.bfloat16

XS, ZS = 4, 8
SW, TW = XS * ZS, 8
DIM = 64
NS, NT = 512, 4096
SUB = NT // SW
TILE = 512
STEP = 128
ROWS = 64
STACK = 80
VECS = 4

(A_COL, A_ROW, A_INIT, A_AGC, A_AGZ, A_AGS, B_COL, B_ROW, B_AGC, B_AGZ, B_AGS, C_SRC, C_TGT,
 D_ROW, D_COL, D_ROW2, D_COL2, O_ROW, O_XX, O_XZ, O_ZF, G_RING1, G_RING2, G_RING3, G_RING4, G_SIB1, G_SIB2) = range(27)
IN_ZF = 27
IN_XF = IN_ZF + ZS
N_SEMS = 27
N_IN = IN_XF + XS
LEAD = 384


def halves(value):
    high = value.astype(BF16)
    return high, (value - high.astype(F32)).astype(BF16)


def across(vector):
    return jnp.broadcast_to(vector, (128, vector.shape[1])).T


def along(block):
    return jnp.sum(block.T, axis=0, keepdims=True)


def tiled(block, times):
    return jnp.concatenate([block] * times, axis=1)


def lane_tiles(value):
    parts = [value[:, k:k + 128] for k in range(0, value.shape[1], 128)]
    while len(parts) > 1:
        parts = [parts[k] + parts[k + 1] for k in range(0, len(parts), 2)]
    return parts[0]


def total(value):
    return jnp.sum(jnp.sum(value, axis=1, keepdims=True), axis=0, keepdims=True)


def lanes(*values):
    spot = lax.broadcasted_iota(jnp.int32, (1, 128), 1)
    row = jnp.zeros((1, 128), F32)
    for index, value in enumerate(values):
        row = row + jnp.where(spot == index, value, 0.0)
    return row


def lane(row, index):
    spot = lax.broadcasted_iota(jnp.int32, (1, 128), 1)
    return jnp.sum(jnp.where(spot == index, row, 0.0), axis=1, keepdims=True)


def kernel(
    shift, xs_hbm, yt_hbm, f_hbm, g_hbm, a0_hbm, b0_hbm,
    sol_src_ref, sol_tgt_ref, gs_ref, gt_ref,
    xs_ref, yt_ref, f_ref, g_ref, a0_ref, b0_ref, load,
    plan, plan_hi, plan_lo, q_hi, q_lo, x4t, y4, fcol, acol, racc, racc2,
    col_a, col_a_in, row_a, row_a_in, init_out, init_in, agc_a, agz_a, ags_a, ags_a_in,
    col_b, col_b_in, row_b, row_b_in, agc_b, agz_b, ags_b_in,
    sc_out, sc_in, sc2_out, sc2_in, ysub, vec_t, vec_s, stack, t_row, t_col,
    g_row, g_row_in, g_col, g_col_in, xg, send, recv,
):
    loads = [
        pltpu.make_async_copy(far, near, load.at[k])
        for k, (far, near) in enumerate((
            (yt_hbm, yt_ref), (xs_hbm, xs_ref), (f_hbm, f_ref), (g_hbm, g_ref), (a0_hbm, a0_ref), (b0_hbm, b0_ref),
        ))
    ]
    for copy in loads:
        copy.start()
    s = lax.axis_index("src")
    t = lax.axis_index("tgt")
    x, z = s // ZS, s % ZS
    core = t % 2
    sibling = (s, t + 1 - 2 * core)

    def src_peer(p):
        return (lax.rem(s + p, SW), t)

    def tgt_peer(p):
        return (s, lax.rem(t + p, TW))

    def z_peer(p):
        return (x * ZS + lax.rem(z + p, ZS), t)

    def x_peer(p):
        return (lax.rem(x + p, XS) * ZS + z, t)

    def push(src, dst, k, device, k_recv=None):
        pltpu.make_async_remote_copy(
            src_ref=src, dst_ref=dst, send_sem=send.at[k],
            recv_sem=recv.at[k if k_recv is None else k_recv],
            device_id=device, device_id_type=MESH,
        ).start()

    def push_all(ways, peer, src, dst, k):
        def step(p, carry):
            push(src(p), dst, k, peer(p))
            return carry
        lax.fori_loop(1, ways, step, 0)

    def wait_in(ref, k):
        pltpu.make_async_copy(ref, ref, recv.at[k]).wait()

    def wait_out(ref, k):
        pltpu.make_async_copy(ref, ref, send.at[k]).wait()

    def sub_of(p):
        return pl.ds(pl.multiple_of(lax.rem(s + p, SW) * SUB, SUB), SUB)

    my_sub = pl.ds(pl.multiple_of(s * SUB, SUB), SUB)
    my_tile = pl.ds(pl.multiple_of(z * TILE, TILE), TILE)

    barrier = pltpu.get_barrier_semaphore()

    def greet(ways, peer):
        def step(p, carry):
            pl.semaphore_signal(barrier, inc=1, device_id=peer(p), device_id_type=MESH)
            return carry
        lax.fori_loop(1, ways, step, 0)

    greet(SW, src_peer)
    greet(TW, tgt_peer)
    for copy in loads[1:]:
        copy.wait()

    xs = jnp.concatenate([xs_ref[0], xs_ref[1]], axis=0)
    a0 = a0_ref[...]
    b0 = b0_ref[...]

    def x_parts(points):
        scaled = points * (LOG2E / EPSILON)
        high = scaled.astype(BF16).astype(F32)
        low = scaled - high
        return jnp.concatenate([high, high, low, low], axis=0).T.astype(BF16)

    x4t[...] = x_parts(xs)

    fcol[...] = across(f_ref[...] * LOG2E + shift)
    acol[...] = across(a0)
    racc[...] = jnp.zeros_like(racc)
    racc2[...] = jnp.zeros_like(racc2)

    loads[0].wait()

    def plan_step(n, carry):
        cs = pl.ds(pl.multiple_of(n * STEP, STEP), STEP)
        high, low = halves(yt_ref[:, cs])
        parts = jnp.concatenate([high, low, high, low], axis=0)
        y4[:, cs] = parts
        cross = jnp.dot(x4t[...], parts, preferred_element_type=F32)
        g_now = g_ref[:, cs] * LOG2E
        b_now = b0_ref[:, cs]
        mass_sum = jnp.zeros((8, STEP), F32)
        a_sum = jnp.zeros((8, STEP), F32)
        for r in range(0, NS, ROWS):
            p = jnp.exp2(cross[r:r + ROWS, :] + tiled(fcol[r:r + ROWS, :], STEP // 128) + g_now)
            plan[r:r + ROWS, cs] = p
            racc[r:r + ROWS, :] += lane_tiles(p)
            racc2[r:r + ROWS, :] += lane_tiles(p * b_now)
            pa = p * tiled(acol[r:r + ROWS, :], STEP // 128)
            mass_sum = mass_sum + jnp.sum(p.reshape(ROWS // 8, 8, STEP), axis=0)
            a_sum = a_sum + jnp.sum(pa.reshape(ROWS // 8, 8, STEP), axis=0)
        col_a[0:1, cs] = jnp.sum(mass_sum, axis=0, keepdims=True)
        col_a[1:2, cs] = jnp.sum(a_sum, axis=0, keepdims=True)
        return carry
    lax.fori_loop(0, NT // STEP, plan_step, 0, unroll=2)

    mass_part = along(racc[...])
    v_part = along(racc2[...])
    row_a[0:1, :] = mass_part
    row_a[1:2, :] = v_part
    init_out[0:1, :] = f_ref[...]
    init_out[1:2, :] = a0
    norm_part = total(a0 * a0) * (1.0 / TW) + total(b0 * b0) * (1.0 / SW)
    quad_part = (
        norm_part * REGULARIZER
        + total(a0 * a0 * mass_part) + total(b0 * b0 * col_a[0:1, :]) + 2.0 * total(a0 * v_part)
    )
    col_a[2:3, :] = tiled(lanes(norm_part, quad_part), SW)
    col_a[3:4, :] = jnp.zeros((1, NT), F32)

    pl.semaphore_wait(barrier, SW - 1 + TW - 1)

    push_all(SW, src_peer, lambda p: col_a.at[:, sub_of(p)], col_a_in.at[s], A_COL)
    push_all(TW, tgt_peer, lambda p: row_a, row_a_in.at[t], A_ROW)
    push_all(ZS, z_peer, lambda p: init_out, init_in.at[z], A_INIT)
    push(xs_ref.at[core], xg.at[z, core], G_RING1, z_peer(1))
    push(xs_ref.at[core], xg.at[z, core], G_RING1, z_peer(ZS - 1))
    col_a_in[s] = col_a[:, my_sub]
    row_a_in[t] = row_a[...]
    init_in[z] = init_out[...]
    xg[z, 0] = xs_ref[0]
    xg[z, 1] = xs_ref[1]
    ysub[...] = yt_ref[:, my_tile]

    g_sub = g_ref[:, my_tile] * LOG2E

    def q_block(p, carry):
        zz = lax.rem(z + p, ZS)
        points = jnp.concatenate([xg[zz, 0], xg[zz, 1]], axis=0)
        fcol[...] = across(init_in[zz][0:1, :] * LOG2E + shift)
        parts = x_parts(points)
        for c in range(0, TILE, 128):
            some = pl.ds(pl.multiple_of(z * TILE + c, 128), 128)
            cross = jnp.dot(parts, y4[:, some], preferred_element_type=F32)
            for r in range(0, NS, 64):
                value = jnp.exp2(cross[r:r + 64, :] + fcol[r:r + 64, :] + g_sub[:, c:c + 128])
                high, low = halves(value)
                q_hi[zz, r:r + 64, c:c + 128] = high
                q_lo[zz, r:r + 64, c:c + 128] = low
        return carry

    def pass_on(p, k):
        before, after = lax.rem(z + ZS - p, ZS), lax.rem(z + p, ZS)
        push(xg.at[before, core], xg.at[before, core], k, z_peer(1))
        push(xg.at[after, core], xg.at[after, core], k, z_peer(ZS - 1))

    def fill_stack(points, weights):
        count = len(weights)
        for v, weight in enumerate(weights):
            value = jnp.concatenate([points * weight, jnp.broadcast_to(weight, (16, TILE))], axis=0)
            high, low = halves(value)
            stack[v * STACK:(v + 1) * STACK, :] = high
            stack[(count + v) * STACK:(count + v + 1) * STACK, :] = low

    def add_sums(out, low, count, plan_high, plan_low, dims):
        rows = count * STACK
        first = lax.dot_general(
            stack[0:2 * rows, :], plan_high, (dims, ((), ())), preferred_element_type=F32
        )
        second = lax.dot_general(
            stack[0:rows, :], plan_low, (dims, ((), ())), preferred_element_type=F32
        )
        out[low * STACK:low * STACK + rows, :] += first[0:rows, :] + first[rows:, :] + second

    def row_sums(low, high, split=False):
        def step(n, carry):
            cs = pl.ds(pl.multiple_of(n * TILE, TILE), TILE)
            if split:
                for r in range(0, NS, 64):
                    top, rest = halves(plan[r:r + 64, cs])
                    plan_hi[r:r + 64, cs] = top
                    plan_lo[r:r + 64, cs] = rest
            fill_stack(yt_ref[:, cs], [vec_t[v:v + 1, cs] for v in range(low, high)])
            add_sums(t_row, low, high - low, plan_hi[:, cs], plan_lo[:, cs], ((1,), (1,)))
            return carry
        lax.fori_loop(0, NT // TILE, step, 0)

    def col_sums(low, high, first=0, last=ZS):
        def step(p, carry):
            zz = lax.rem(z + p, ZS)
            fill_stack(
                jnp.concatenate([xg[zz, 0], xg[zz, 1]], axis=0),
                [vec_s[zz, v:v + 1, :] for v in range(low, high)],
            )
            add_sums(t_col, low, high - low, q_hi[zz], q_lo[zz], ((1,), (0,)))
            return carry
        lax.fori_loop(first, last, step, 0)

    t_row[...] = jnp.zeros_like(t_row)
    t_col[...] = jnp.zeros_like(t_col)
    vec_t[0:1, :] = jnp.ones((1, NT), F32)
    vec_t[1:2, :] = b0
    vec_s[:, 0, :] = jnp.ones((ZS, NS), F32)
    row_sums(0, 2, split=True)
    wait_in(xg.at[pl.ds(0, 2), 0], G_RING1)
    pass_on(1, G_RING2)

    wait_in(row_a_in.at[pl.ds(0, TW - 1)], A_ROW)
    row_full = jnp.sum(row_a_in[...], axis=0)
    agz_own = row_full
    wait_in(col_a_in.at[pl.ds(0, SW - 1)], A_COL)
    col_full = jnp.sum(col_a_in[...], axis=0)
    agc_a[:, my_sub] = col_full[0:2, :]
    ags_a[...] = col_full[2:3, :]
    agz_a[z] = agz_own

    push_all(SW, src_peer, lambda p: agc_a.at[:, my_sub], agc_a.at[:, my_sub], A_AGC)
    push_all(TW, tgt_peer, lambda p: ags_a, ags_a_in.at[t], A_AGS)
    push_all(ZS, z_peer, lambda p: agz_a.at[z], agz_a.at[z], A_AGZ)
    ags_a_in[t] = ags_a[...]
    wait_in(init_in.at[pl.ds(0, ZS - 1)], A_INIT)
    wait_in(xg.at[pl.ds(0, 2), 0], G_RING2)
    pass_on(2, G_RING3)
    for p in (1, ZS - 1, 2, ZS - 2):
        zz = lax.rem(z + p, ZS)
        push(xg.at[zz, core], xg.at[zz, core], G_SIB1, sibling)
    q_block(0, 0)
    wait_in(xg.at[pl.ds(0, 4), 0], G_SIB1)
    lax.fori_loop(1, 3, q_block, 0)
    lax.fori_loop(6, 8, q_block, 0)

    wait_in(agz_a.at[pl.ds(0, ZS - 1)], A_AGZ)
    wait_in(ags_a_in.at[pl.ds(0, TW - 1)], A_AGS)
    wait_in(agc_a.at[:, pl.ds(0, (SW - 1) * SUB)], A_AGC)
    sums = jnp.sum(ags_a_in[...], axis=0)
    norm0 = lane(sums, 0)
    alpha0 = norm0 / lane(sums, 1)

    diag = [row_full[0:1, :] + REGULARIZER, agz_a[:, 0, :] + REGULARIZER, agc_a[0:1, :] + REGULARIZER]
    res0 = [a0, init_in[:, 1, :], b0]
    prod0 = [row_full[1:2, :], agz_a[:, 1, :], agc_a[1:2, :]]
    image0 = [d * r + v for d, r, v in zip(diag, res0, prod0)]
    res1 = [r - alpha0 * i for r, i in zip(res0, image0)]

    def matvec(vec_src, vec_tgt, columns):
        acol[...] = across(vec_src)
        half = NT // 2
        for h, acc in ((0, racc), (1, racc2)):
            spread = jnp.broadcast_to(vec_tgt[:, h * half:(h + 1) * half], (8, half))

            def step(r, sums):
                rows = pl.ds(pl.multiple_of(r * 8, 8), 8)
                p = plan[rows, h * half:(h + 1) * half]
                terms = p * spread
                parts = [terms[:, k * 128:(k + 1) * 128] for k in range(half // 128)]
                while len(parts) > 1:
                    parts = [parts[k] + parts[k + 1] for k in range(0, len(parts), 2)]
                acc[rows, :] = parts[0]
                if columns:
                    sums = sums + p * tiled(acol[rows, :], half // 128)
                return sums
            sums = lax.fori_loop(0, NS // 8, step, jnp.zeros((8, half), F32), unroll=2)
            if columns:
                col_b[0:1, h * half:(h + 1) * half] = jnp.sum(sums, axis=0, keepdims=True)
        return along(racc[...] + racc2[...])

    def scalars(res, row_part):
        norm = total(res[0] * res[0]) * (1.0 / TW) + total(res[2] * res[2]) * (1.0 / SW)
        quad = (
            total(res[0] * res[0] * diag[0]) * (1.0 / TW)
            + total(res[2] * res[2] * diag[2]) * (1.0 / SW)
            + 2.0 * total(res[0] * row_part)
        )
        return lanes(norm, quad)

    row_part = matvec(res1[0], res1[2], True)
    row_b[...] = row_part
    col_b[1:2, :] = tiled(scalars(res1, row_part), SW)

    push_all(SW, src_peer, lambda p: col_b.at[:, sub_of(p)], col_b_in.at[s], B_COL)
    push_all(TW, tgt_peer, lambda p: row_b, row_b_in.at[t], B_ROW)
    col_b_in[s] = col_b[:, my_sub]
    row_b_in[t] = row_b[...]
    wait_in(xg.at[pl.ds(0, 2), 0], G_RING3)
    before, after = lax.rem(z + ZS - 3, ZS), lax.rem(z + 3, ZS)
    top, rest = pl.ds(0, 16), pl.ds(16, 16)
    push(xg.at[before, core, top], xg.at[before, core, top], G_RING4, z_peer(1))
    push(xg.at[after, core, rest], xg.at[after, core, rest], G_RING4, z_peer(ZS - 1))
    vec_t[2:3, :] = res1[2]
    vec_s[:, 1, :] = res0[1]
    vec_s[:, 2, :] = res1[1]
    row_sums(2, 3)
    col_sums(0, 3, 0, 3)
    col_sums(0, 3, 6, 8)

    wait_in(row_b_in.at[pl.ds(0, TW - 1)], B_ROW)
    row_full1 = jnp.sum(row_b_in[...], axis=0)
    agz_b[z] = row_full1
    wait_in(col_b_in.at[pl.ds(0, SW - 1)], B_COL)
    col_full1 = jnp.sum(col_b_in[...], axis=0)
    agc_b[:, my_sub] = col_full1[0:1, :]
    sc2_out[0] = col_full1[1:2, :]

    push_all(SW, src_peer, lambda p: agc_b.at[:, my_sub], agc_b.at[:, my_sub], B_AGC)
    push_all(TW, tgt_peer, lambda p: sc2_out.at[0], ags_b_in.at[t], B_AGS)
    push_all(ZS, z_peer, lambda p: agz_b.at[z], agz_b.at[z], B_AGZ)
    ags_b_in[t] = sc2_out[0]
    wait_in(xg.at[0, 0], G_RING4)
    for p in (3, ZS - 3, 4):
        zz = lax.rem(z + p, ZS)
        push(xg.at[zz, core], xg.at[zz, core], G_SIB2, sibling)
    wait_in(xg.at[pl.ds(0, 3), 0], G_SIB2)
    lax.fori_loop(3, 6, q_block, 0)
    col_sums(0, 3, 3, 6)

    wait_in(agz_b.at[pl.ds(0, ZS - 1)], B_AGZ)
    wait_in(ags_b_in.at[pl.ds(0, TW - 1)], B_AGS)
    wait_in(agc_b.at[:, pl.ds(0, (SW - 1) * SUB)], B_AGC)
    sums = jnp.sum(ags_b_in[...], axis=0)
    norm1 = lane(sums, 0)
    beta0 = norm1 / norm0
    alpha1 = norm1 / (lane(sums, 1) - beta0 * norm1 / alpha0)
    prod1 = [row_full1, agz_b[:, 0, :], agc_b[...]]
    dir1 = [r1 + beta0 * r0 for r1, r0 in zip(res1, res0)]
    image1 = [d * r + v + beta0 * i for d, r, v, i in zip(diag, res1, prod1, image0)]
    res2 = [r - alpha1 * i for r, i in zip(res1, image1)]
    sol2 = [alpha0 * r0 + alpha1 * d1 for r0, d1 in zip(res0, dir1)]

    row_part = matvec(res2[0], res2[2], False)
    sc_out[...] = scalars(res2, row_part)

    push_all(SW, src_peer, lambda p: sc_out, sc_in.at[s], C_SRC)
    sc_in[s] = sc_out[...]

    vec_t[3:4, :] = res2[2]
    vec_s[:, 3, :] = res2[1]
    first_step = alpha0 + alpha1 * beta0

    def sums_of(points, out, v):
        low = v * STACK
        return points * out[low + 64:low + 65, :] - out[low:low + 64, :]

    def early_gradients(points, out, own, write):
        ones = sums_of(points, out, 0)
        zeroth = sums_of(points, out, 1)
        latest = sums_of(points, out, 2)
        write(0, (1.0 + first_step * own[0] + alpha1 * own[1]) * ones + first_step * zeroth + alpha1 * latest)
        write(1, (own[1] + beta0 * own[0]) * ones + latest + beta0 * zeroth)

    def late_gradient(points, out, own, write):
        write(2, own[2] * sums_of(points, out, 0) + sums_of(points, out, 3))

    def write_col(part, value):
        for k in range(XS):
            g_col[part, k] = value[k * 16:(k + 1) * 16, :]

    def write_row(part, value):
        for k in range(TW):
            g_row[part, k] = value[k * 8:(k + 1) * 8, :]

    early, late = pl.ds(0, 2), pl.ds(2, 1)
    own_t = vec_t[:, my_tile]
    own_t = [own_t[v:v + 1, :] for v in range(1, VECS)]
    own_s = [res0[0], res1[0], res2[0]]
    early_gradients(ysub[...], t_col, own_t, write_col)
    push_all(XS, x_peer, lambda p: g_col.at[early, lax.rem(x + p, XS)], g_col_in.at[x, early], D_COL)
    early_gradients(xs, t_row, own_s, write_row)
    push_all(TW, tgt_peer, lambda p: g_row.at[early, lax.rem(t + p, TW)], g_row_in.at[t, early], D_ROW)
    col_sums(3, 4)
    late_gradient(ysub[...], t_col, own_t, write_col)
    push_all(XS, x_peer, lambda p: g_col.at[late, lax.rem(x + p, XS)], g_col_in.at[x, late], D_COL2)
    g_col_in[x] = g_col[:, x]
    wait_in(sc_in.at[pl.ds(0, SW - 1)], C_SRC)
    sc2_out[1] = jnp.sum(sc_in[...], axis=0)
    push_all(TW, tgt_peer, lambda p: sc2_out.at[1], sc2_in.at[t], C_TGT)
    sc2_in[t] = sc2_out[1]

    row_sums(3, 4)
    late_gradient(xs, t_row, own_s, write_row)
    push_all(TW, tgt_peer, lambda p: g_row.at[late, lax.rem(t + p, TW)], g_row_in.at[t, late], D_ROW2)
    g_row_in[t] = g_row[:, t]

    wait_in(sc2_in.at[pl.ds(0, TW - 1)], C_TGT)
    sums = jnp.sum(sc2_in[...], axis=0)
    norm2 = lane(sums, 0)
    beta1 = norm2 / norm1
    alpha2 = norm2 / (lane(sums, 1) - beta1 * norm2 / alpha1)
    both = alpha2 * beta1

    def combine(parts):
        return (parts[0] + both * parts[1] + alpha2 * parts[2]) * (1.0 / EPSILON)

    def lead_of(zz):
        return pl.ds(pl.multiple_of(zz * TILE, TILE), LEAD)

    def rest_of(zz):
        return pl.ds(pl.multiple_of(zz * TILE + LEAD, 128), TILE - LEAD)

    wait_in(g_col_in.at[pl.ds(0, XS - 1), early], D_COL)
    wait_in(g_col_in.at[pl.ds(0, XS - 1), late], D_COL2)
    gt_ref[x, :, my_tile] = combine(jnp.sum(g_col_in[...], axis=0))
    mine = gt_ref.at[x, :, rest_of(z)]
    push_all(XS, x_peer, lambda p: mine, mine, O_XX)
    for p in (1, ZS - 1, 2, ZS - 2, 3, ZS - 3, 4):
        push(gt_ref.at[x, :, lead_of(z)], gt_ref.at[x, :, lead_of(z)], O_ZF, z_peer(p), IN_ZF + p)

    def lead_along_x(zz):
        for p in range(1, XS):
            push(gt_ref.at[x, :, lead_of(zz)], gt_ref.at[x, :, lead_of(zz)], O_ZF, x_peer(p), IN_XF + p)

    lead_along_x(z)

    sol_src_ref[...] = sol2[0] + both * dir1[0] + alpha2 * res2[0]
    sol_tgt_ref[...] = sol2[2] + both * dir1[2] + alpha2 * res2[2]

    wait_in(gt_ref.at[pl.ds(0, XS - 1), :, pl.ds(0, TILE - LEAD)], O_XX)
    push_all(
        ZS, z_peer, lambda p: gt_ref.at[:, :, rest_of(z)], gt_ref.at[:, :, rest_of(z)], O_XZ
    )
    for p in (1, ZS - 1, 2, ZS - 2, 3, ZS - 3, 4):
        zz = lax.rem(z + ZS - p, ZS)
        wait_in(gt_ref.at[x, :, lead_of(zz)], IN_ZF + p)
        lead_along_x(zz)
        if p == ZS - 1:
            wait_in(g_row_in.at[pl.ds(0, TW - 1), early], D_ROW)
            wait_in(g_row_in.at[pl.ds(0, TW - 1), late], D_ROW2)
            gs_ref[t] = combine(jnp.sum(g_row_in[...], axis=0))
            push_all(TW, tgt_peer, lambda p: gs_ref.at[t], gs_ref.at[t], O_ROW)

    wait_in(gs_ref.at[pl.ds(0, TW - 1)], O_ROW)
    wait_in(gt_ref.at[:, :, pl.ds(0, (ZS - 1) * (TILE - LEAD))], O_XZ)
    for p in range(1, XS):
        wait_in(gt_ref.at[0, :, pl.ds(0, ZS * LEAD)], IN_XF + p)

    wait_out(col_a_in.at[pl.ds(0, SW - 1)], A_COL)
    wait_out(row_a_in.at[pl.ds(0, TW - 1)], A_ROW)
    wait_out(init_in.at[pl.ds(0, ZS - 1)], A_INIT)
    wait_out(agc_a.at[:, pl.ds(0, (SW - 1) * SUB)], A_AGC)
    wait_out(agz_a.at[pl.ds(0, ZS - 1)], A_AGZ)
    wait_out(ags_a_in.at[pl.ds(0, TW - 1)], A_AGS)
    wait_out(col_b_in.at[pl.ds(0, SW - 1)], B_COL)
    wait_out(row_b_in.at[pl.ds(0, TW - 1)], B_ROW)
    wait_out(agc_b.at[:, pl.ds(0, (SW - 1) * SUB)], B_AGC)
    wait_out(agz_b.at[pl.ds(0, ZS - 1)], B_AGZ)
    wait_out(ags_b_in.at[pl.ds(0, TW - 1)], B_AGS)
    wait_out(sc_in.at[pl.ds(0, SW - 1)], C_SRC)
    wait_out(sc2_in.at[pl.ds(0, TW - 1)], C_TGT)
    wait_out(g_row_in.at[pl.ds(0, TW - 1), early], D_ROW)
    wait_out(g_col_in.at[pl.ds(0, XS - 1), early], D_COL)
    wait_out(g_row_in.at[pl.ds(0, TW - 1), late], D_ROW2)
    wait_out(g_col_in.at[pl.ds(0, XS - 1), late], D_COL2)
    wait_out(gs_ref.at[pl.ds(0, TW - 1)], O_ROW)
    wait_out(gt_ref.at[pl.ds(0, XS - 1), :, pl.ds(0, TILE - LEAD)], O_XX)
    wait_out(gt_ref.at[:, :, pl.ds(0, (ZS - 1) * (TILE - LEAD))], O_XZ)
    wait_out(gt_ref.at[pl.ds(0, 3), :, pl.ds(0, ZS * LEAD)], O_ZF)
    wait_out(gt_ref.at[0, :, pl.ds(0, (ZS - 1) * LEAD)], O_ZF)
    for k in (G_RING1, G_RING2, G_RING3):
        wait_out(xg.at[pl.ds(0, 2), 0], k)
    wait_out(xg.at[0, 0], G_RING4)
    wait_out(xg.at[pl.ds(0, 4), 0], G_SIB1)
    wait_out(xg.at[pl.ds(0, 3), 0], G_SIB2)


def hand_out(*refs):
    sems = refs[-1]
    parts = [(refs[3].at[k], refs[7].at[k], refs[11].at[k]) for k in range(XS)]
    parts += [(refs[k], refs[4 + k], refs[8 + k]) for k in (2, 1, 0)]
    loads = [pltpu.make_async_copy(src, near, sems.at[k]) for k, (src, _, near) in enumerate(parts)]
    stores = [
        pltpu.make_async_copy(near, dst, sems.at[len(parts) + k])
        for k, (_, dst, near) in enumerate(parts)
    ]
    for load in loads:
        load.start()
    for load, store in zip(loads, stores):
        load.wait()
        store.start()
    for store in stores:
        store.wait()


def body(src_points, tgt_points, src_potential, tgt_potential, src_rhs, tgt_rhs):
    normalizer = 1.0 / math.sqrt(NS * SW * NT * TW)
    vmem = pl.BlockSpec(memory_space=pltpu.VMEM)
    far = pl.BlockSpec(memory_space=pltpu.HBM)

    def buf(*shape, dtype=F32):
        return pltpu.VMEM(shape, dtype)

    scratch = [
        buf(2, DIM // 2, NS), buf(DIM, NT), buf(1, NS), buf(1, NT), buf(1, NS), buf(1, NT),
        pltpu.SemaphoreType.DMA((6,)),
        buf(NS, NT), buf(NS, NT, dtype=BF16), buf(NS, NT, dtype=BF16),
        buf(ZS, NS, TILE, dtype=BF16), buf(ZS, NS, TILE, dtype=BF16),
        buf(NS, 256, dtype=BF16), buf(256, NT, dtype=BF16),
        buf(NS, 128), buf(NS, 128), buf(NS, 128), buf(NS, 128),
        buf(4, NT), buf(SW, 4, SUB), buf(2, NS), buf(TW, 2, NS),
        buf(2, NS), buf(ZS, 2, NS),
        buf(2, NT), buf(ZS, 2, NS), buf(1, 128), buf(TW, 1, 128),
        buf(2, NT), buf(SW, 2, SUB), buf(1, NS), buf(TW, 1, NS),
        buf(1, NT), buf(ZS, 1, NS), buf(TW, 1, 128),
        buf(1, 128), buf(SW, 1, 128), buf(2, 1, 128), buf(TW, 1, 128),
        buf(DIM, TILE), buf(VECS, NT), buf(ZS, VECS, NS),
        buf(2 * 3 * STACK, TILE, dtype=BF16),
        buf(VECS * STACK, NS), buf(VECS * STACK, TILE),
        buf(3, TW, 8, NS), buf(TW, 3, 8, NS),
        buf(3, XS, 16, TILE), buf(XS, 3, 16, TILE),
        buf(ZS, 2, DIM // 2, NS),
        pltpu.SemaphoreType.DMA((N_SEMS,)), pltpu.SemaphoreType.DMA((N_IN,)),
    ]
    shapes = (
        jax.ShapeDtypeStruct((1, NS), F32),
        jax.ShapeDtypeStruct((1, NT), F32),
        jax.ShapeDtypeStruct((TW, 8, NS), F32),
        jax.ShapeDtypeStruct((XS, 16, NT), F32),
    )
    results = pl.pallas_call(
        functools.partial(kernel, math.log2(normalizer)),
        out_shape=shapes,
        in_specs=[far] * 6,
        out_specs=[vmem] * 4,
        scratch_shapes=scratch,
        compiler_params=pltpu.CompilerParams(
            collective_id=1, has_side_effects=True, vmem_limit_bytes=60 * 1024 * 1024
        ),
    )(
        src_points.reshape(2, DIM // 2, NS), tgt_points, src_potential.reshape(1, NS),
        tgt_potential.reshape(1, NT), src_rhs.reshape(1, NS), tgt_rhs.reshape(1, NT),
    )
    sol_src, sol_tgt, grad_src, grad_tgt = pl.pallas_call(
        hand_out,
        out_shape=shapes,
        in_specs=[far] * 4,
        out_specs=[far] * 4,
        scratch_shapes=[buf(*shape.shape) for shape in shapes] + [pltpu.SemaphoreType.DMA((2 * (XS + 3),))],
        compiler_params=pltpu.CompilerParams(vmem_limit_bytes=60 * 1024 * 1024),
    )(*results)
    return (
        sol_src.reshape(NS), sol_tgt.reshape(NT), grad_src.reshape(DIM, NS), grad_tgt.reshape(DIM, NT)
    )


def solution(mesh):
    return jax.shard_map(
        body,
        mesh=mesh,
        in_specs=(P(None, "src"), P(None, "tgt"), P("src"), P("tgt"), P("src"), P("tgt")),
        out_specs=(P("src"), P("tgt"), P(None, "src"), P(None, "tgt")),
        check_vma=False,
    )
```

```python
import functools
import math

import jax
import jax.numpy as jnp
from jax import lax
from jax.experimental import pallas as pl
from jax.experimental.pallas import tpu as pltpu
from jax.sharding import PartitionSpec as P

EPSILON = 0.5
REGULARIZER = 1.0
LOG2E = math.log2(math.e)
MESH = pl.DeviceIdType.MESH
F32 = jnp.float32
BF16 = jnp.bfloat16

XS, ZS = 4, 8
SW, TW = XS * ZS, 8
DIM = 64
NS, NT = 512, 4096
SUB = NT // SW
TILE = 512
STEP = 256
ROWS = 64
STACK = 80
VECS = 4

(A_COL, A_ROW, A_INIT, A_AGC, A_AGZ, A_AGS, B_COL, B_ROW, B_AGC, B_AGZ, B_AGS, C_SRC, C_TGT,
 D_ROW, D_COL, D_ROW2, D_COL2, O_ROW, O_XX, O_XZ, O_ZF, G_RING1, G_RING2, G_RING3, G_RING4, G_SIB1, G_SIB2) = range(27)
IN_ZF = 27
IN_XF = IN_ZF + ZS
N_SEMS = 27
N_IN = IN_XF + XS
LEAD = 384


def halves(value):
    high = value.astype(BF16)
    return high, (value - high.astype(F32)).astype(BF16)


def across(vector):
    return jnp.broadcast_to(vector, (128, vector.shape[1])).T


def along(block):
    return jnp.sum(block.T, axis=0, keepdims=True)


def tiled(block, times):
    return jnp.concatenate([block] * times, axis=1)


def lane_tiles(value):
    parts = [value[:, k:k + 128] for k in range(0, value.shape[1], 128)]
    while len(parts) > 1:
        parts = [parts[k] + parts[k + 1] for k in range(0, len(parts), 2)]
    return parts[0]


def total(value):
    return jnp.sum(jnp.sum(value, axis=1, keepdims=True), axis=0, keepdims=True)


def lanes(*values):
    spot = lax.broadcasted_iota(jnp.int32, (1, 128), 1)
    row = jnp.zeros((1, 128), F32)
    for index, value in enumerate(values):
        row = row + jnp.where(spot == index, value, 0.0)
    return row


def lane(row, index):
    spot = lax.broadcasted_iota(jnp.int32, (1, 128), 1)
    return jnp.sum(jnp.where(spot == index, row, 0.0), axis=1, keepdims=True)


def kernel(
    shift, xs_hbm, yt_hbm, f_hbm, g_hbm, a0_hbm, b0_hbm,
    sol_src_ref, sol_tgt_ref, gs_ref, gt_ref,
    xs_ref, yt_ref, f_ref, g_ref, a0_ref, b0_ref, load,
    plan, plan_hi, plan_lo, q_hi, q_lo, x4t, y4, fcol, acol, racc, racc2,
    col_a, col_a_in, row_a, row_a_in, init_out, init_in, agc_a, agz_a, ags_a, ags_a_in,
    col_b, col_b_in, row_b, row_b_in, agc_b, agz_b, ags_b_in,
    sc_out, sc_in, sc2_out, sc2_in, ysub, vec_t, vec_s, stack, t_row, t_col,
    g_row, g_row_in, g_col, g_col_in, xg, send, recv,
):
    loads = [
        pltpu.make_async_copy(far, near, load.at[k])
        for k, (far, near) in enumerate((
            (yt_hbm, yt_ref), (xs_hbm, xs_ref), (f_hbm, f_ref), (g_hbm, g_ref), (a0_hbm, a0_ref), (b0_hbm, b0_ref),
        ))
    ]
    for copy in loads:
        copy.start()
    s = lax.axis_index("src")
    t = lax.axis_index("tgt")
    x, z = s // ZS, s % ZS
    core = t % 2
    sibling = (s, t + 1 - 2 * core)

    def src_peer(p):
        return (lax.rem(s + p, SW), t)

    def tgt_peer(p):
        return (s, lax.rem(t + p, TW))

    def z_peer(p):
        return (x * ZS + lax.rem(z + p, ZS), t)

    def x_peer(p):
        return (lax.rem(x + p, XS) * ZS + z, t)

    def push(src, dst, k, device, k_recv=None):
        pltpu.make_async_remote_copy(
            src_ref=src, dst_ref=dst, send_sem=send.at[k],
            recv_sem=recv.at[k if k_recv is None else k_recv],
            device_id=device, device_id_type=MESH,
        ).start()

    def push_all(ways, peer, src, dst, k):
        def step(p, carry):
            push(src(p), dst, k, peer(p))
            return carry
        lax.fori_loop(1, ways, step, 0)

    def wait_in(ref, k):
        pltpu.make_async_copy(ref, ref, recv.at[k]).wait()

    def wait_out(ref, k):
        pltpu.make_async_copy(ref, ref, send.at[k]).wait()

    def sub_of(p):
        return pl.ds(pl.multiple_of(lax.rem(s + p, SW) * SUB, SUB), SUB)

    my_sub = pl.ds(pl.multiple_of(s * SUB, SUB), SUB)
    my_tile = pl.ds(pl.multiple_of(z * TILE, TILE), TILE)

    barrier = pltpu.get_barrier_semaphore()

    def greet(ways, peer):
        def step(p, carry):
            pl.semaphore_signal(barrier, inc=1, device_id=peer(p), device_id_type=MESH)
            return carry
        lax.fori_loop(1, ways, step, 0)

    greet(SW, src_peer)
    greet(TW, tgt_peer)
    for copy in loads[1:]:
        copy.wait()

    xs = jnp.concatenate([xs_ref[0], xs_ref[1]], axis=0)
    a0 = a0_ref[...]
    b0 = b0_ref[...]

    def x_parts(points):
        scaled = points * (LOG2E / EPSILON)
        high = scaled.astype(BF16).astype(F32)
        low = scaled - high
        return jnp.concatenate([high, high, low, low], axis=0).T.astype(BF16)

    x4t[...] = x_parts(xs)

    fcol[...] = across(f_ref[...] * LOG2E + shift)
    acol[...] = across(a0)
    racc[...] = jnp.zeros_like(racc)
    racc2[...] = jnp.zeros_like(racc2)

    loads[0].wait()

    def plan_step(n, carry):
        cs = pl.ds(pl.multiple_of(n * STEP, STEP), STEP)
        high, low = halves(yt_ref[:, cs])
        parts = jnp.concatenate([high, low, high, low], axis=0)
        y4[:, cs] = parts
        cross = jnp.dot(x4t[...], parts, preferred_element_type=F32)
        g_now = g_ref[:, cs] * LOG2E
        b_now = b0_ref[:, cs]
        mass_sum = jnp.zeros((8, STEP), F32)
        a_sum = jnp.zeros((8, STEP), F32)
        for r in range(0, NS, ROWS):
            p = jnp.exp2(cross[r:r + ROWS, :] + tiled(fcol[r:r + ROWS, :], STEP // 128) + g_now)
            plan[r:r + ROWS, cs] = p
            racc[r:r + ROWS, :] += lane_tiles(p)
            racc2[r:r + ROWS, :] += lane_tiles(p * b_now)
            pa = p * tiled(acol[r:r + ROWS, :], STEP // 128)
            mass_sum = mass_sum + jnp.sum(p.reshape(ROWS // 8, 8, STEP), axis=0)
            a_sum = a_sum + jnp.sum(pa.reshape(ROWS // 8, 8, STEP), axis=0)
        col_a[0:1, cs] = jnp.sum(mass_sum, axis=0, keepdims=True)
        col_a[1:2, cs] = jnp.sum(a_sum, axis=0, keepdims=True)
        return carry
    lax.fori_loop(0, NT // STEP, plan_step, 0)

    mass_part = along(racc[...])
    v_part = along(racc2[...])
    row_a[0:1, :] = mass_part
    row_a[1:2, :] = v_part
    init_out[0:1, :] = f_ref[...]
    init_out[1:2, :] = a0
    norm_part = total(a0 * a0) * (1.0 / TW) + total(b0 * b0) * (1.0 / SW)
    quad_part = (
        norm_part * REGULARIZER
        + total(a0 * a0 * mass_part) + total(b0 * b0 * col_a[0:1, :]) + 2.0 * total(a0 * v_part)
    )
    col_a[2:3, :] = tiled(lanes(norm_part, quad_part), SW)
    col_a[3:4, :] = jnp.zeros((1, NT), F32)

    pl.semaphore_wait(barrier, SW - 1 + TW - 1)

    push_all(SW, src_peer, lambda p: col_a.at[:, sub_of(p)], col_a_in.at[s], A_COL)
    push_all(TW, tgt_peer, lambda p: row_a, row_a_in.at[t], A_ROW)
    push_all(ZS, z_peer, lambda p: init_out, init_in.at[z], A_INIT)
    push(xs_ref.at[core], xg.at[z, core], G_RING1, z_peer(1))
    push(xs_ref.at[core], xg.at[z, core], G_RING1, z_peer(ZS - 1))
    col_a_in[s] = col_a[:, my_sub]
    row_a_in[t] = row_a[...]
    init_in[z] = init_out[...]
    xg[z, 0] = xs_ref[0]
    xg[z, 1] = xs_ref[1]
    ysub[...] = yt_ref[:, my_tile]

    g_sub = g_ref[:, my_tile] * LOG2E

    def q_block(p, carry):
        zz = lax.rem(z + p, ZS)
        points = jnp.concatenate([xg[zz, 0], xg[zz, 1]], axis=0)
        fcol[...] = across(init_in[zz][0:1, :] * LOG2E + shift)
        cross = jnp.dot(x_parts(points), y4[:, my_tile], preferred_element_type=F32)
        for r in range(0, NS, 64):
            value = jnp.exp2(cross[r:r + 64, :] + tiled(fcol[r:r + 64, :], 4) + g_sub)
            high, low = halves(value)
            q_hi[zz, r:r + 64, :] = high
            q_lo[zz, r:r + 64, :] = low
        return carry

    def pass_on(p, k):
        before, after = lax.rem(z + ZS - p, ZS), lax.rem(z + p, ZS)
        push(xg.at[before, core], xg.at[before, core], k, z_peer(1))
        push(xg.at[after, core], xg.at[after, core], k, z_peer(ZS - 1))

    def fill_stack(points, weights):
        count = len(weights)
        for v, weight in enumerate(weights):
            value = jnp.concatenate([points * weight, jnp.broadcast_to(weight, (16, TILE))], axis=0)
            high, low = halves(value)
            stack[v * STACK:(v + 1) * STACK, :] = high
            stack[(count + v) * STACK:(count + v + 1) * STACK, :] = low

    def add_sums(out, low, count, plan_high, plan_low, dims):
        rows = count * STACK
        first = lax.dot_general(
            stack[0:2 * rows, :], plan_high, (dims, ((), ())), preferred_element_type=F32
        )
        second = lax.dot_general(
            stack[0:rows, :], plan_low, (dims, ((), ())), preferred_element_type=F32
        )
        out[low * STACK:low * STACK + rows, :] += first[0:rows, :] + first[rows:, :] + second

    def row_sums(low, high, split=False):
        def step(n, carry):
            cs = pl.ds(pl.multiple_of(n * TILE, TILE), TILE)
            if split:
                for r in range(0, NS, 64):
                    top, rest = halves(plan[r:r + 64, cs])
                    plan_hi[r:r + 64, cs] = top
                    plan_lo[r:r + 64, cs] = rest
            fill_stack(yt_ref[:, cs], [vec_t[v:v + 1, cs] for v in range(low, high)])
            add_sums(t_row, low, high - low, plan_hi[:, cs], plan_lo[:, cs], ((1,), (1,)))
            return carry
        lax.fori_loop(0, NT // TILE, step, 0)

    def col_sums(low, high, first=0, last=ZS):
        def step(p, carry):
            zz = lax.rem(z + p, ZS)
            fill_stack(
                jnp.concatenate([xg[zz, 0], xg[zz, 1]], axis=0),
                [vec_s[zz, v:v + 1, :] for v in range(low, high)],
            )
            add_sums(t_col, low, high - low, q_hi[zz], q_lo[zz], ((1,), (0,)))
            return carry
        lax.fori_loop(first, last, step, 0)

    t_row[...] = jnp.zeros_like(t_row)
    t_col[...] = jnp.zeros_like(t_col)
    vec_t[0:1, :] = jnp.ones((1, NT), F32)
    vec_t[1:2, :] = b0
    vec_s[:, 0, :] = jnp.ones((ZS, NS), F32)
    row_sums(0, 2, split=True)
    wait_in(xg.at[pl.ds(0, 2), 0], G_RING1)
    pass_on(1, G_RING2)

    wait_in(row_a_in.at[pl.ds(0, TW - 1)], A_ROW)
    row_full = jnp.sum(row_a_in[...], axis=0)
    agz_own = row_full
    wait_in(col_a_in.at[pl.ds(0, SW - 1)], A_COL)
    col_full = jnp.sum(col_a_in[...], axis=0)
    agc_a[:, my_sub] = col_full[0:2, :]
    ags_a[...] = col_full[2:3, :]
    agz_a[z] = agz_own

    push_all(SW, src_peer, lambda p: agc_a.at[:, my_sub], agc_a.at[:, my_sub], A_AGC)
    push_all(TW, tgt_peer, lambda p: ags_a, ags_a_in.at[t], A_AGS)
    push_all(ZS, z_peer, lambda p: agz_a.at[z], agz_a.at[z], A_AGZ)
    ags_a_in[t] = ags_a[...]
    wait_in(init_in.at[pl.ds(0, ZS - 1)], A_INIT)
    wait_in(xg.at[pl.ds(0, 2), 0], G_RING2)
    pass_on(2, G_RING3)
    for p in (1, ZS - 1, 2, ZS - 2):
        zz = lax.rem(z + p, ZS)
        push(xg.at[zz, core], xg.at[zz, core], G_SIB1, sibling)
    q_block(0, 0)
    wait_in(xg.at[pl.ds(0, 4), 0], G_SIB1)
    lax.fori_loop(1, 3, q_block, 0)
    lax.fori_loop(6, 8, q_block, 0)

    wait_in(agz_a.at[pl.ds(0, ZS - 1)], A_AGZ)
    wait_in(ags_a_in.at[pl.ds(0, TW - 1)], A_AGS)
    wait_in(agc_a.at[:, pl.ds(0, (SW - 1) * SUB)], A_AGC)
    sums = jnp.sum(ags_a_in[...], axis=0)
    norm0 = lane(sums, 0)
    alpha0 = norm0 / lane(sums, 1)

    diag = [row_full[0:1, :] + REGULARIZER, agz_a[:, 0, :] + REGULARIZER, agc_a[0:1, :] + REGULARIZER]
    res0 = [a0, init_in[:, 1, :], b0]
    prod0 = [row_full[1:2, :], agz_a[:, 1, :], agc_a[1:2, :]]
    image0 = [d * r + v for d, r, v in zip(diag, res0, prod0)]
    res1 = [r - alpha0 * i for r, i in zip(res0, image0)]

    def matvec(vec_src, vec_tgt, columns):
        acol[...] = across(vec_src)
        half = NT // 2
        for h, acc in ((0, racc), (1, racc2)):
            spread = jnp.broadcast_to(vec_tgt[:, h * half:(h + 1) * half], (8, half))

            def step(r, sums):
                rows = pl.ds(pl.multiple_of(r * 8, 8), 8)
                p = plan[rows, h * half:(h + 1) * half]
                terms = p * spread
                parts = [terms[:, k * 128:(k + 1) * 128] for k in range(half // 128)]
                while len(parts) > 1:
                    parts = [parts[k] + parts[k + 1] for k in range(0, len(parts), 2)]
                acc[rows, :] = parts[0]
                if columns:
                    sums = sums + p * tiled(acol[rows, :], half // 128)
                return sums
            sums = lax.fori_loop(0, NS // 8, step, jnp.zeros((8, half), F32), unroll=2)
            if columns:
                col_b[0:1, h * half:(h + 1) * half] = jnp.sum(sums, axis=0, keepdims=True)
        return along(racc[...] + racc2[...])

    def scalars(res, row_part):
        norm = total(res[0] * res[0]) * (1.0 / TW) + total(res[2] * res[2]) * (1.0 / SW)
        quad = (
            total(res[0] * res[0] * diag[0]) * (1.0 / TW)
            + total(res[2] * res[2] * diag[2]) * (1.0 / SW)
            + 2.0 * total(res[0] * row_part)
        )
        return lanes(norm, quad)

    row_part = matvec(res1[0], res1[2], True)
    row_b[...] = row_part
    col_b[1:2, :] = tiled(scalars(res1, row_part), SW)

    push_all(SW, src_peer, lambda p: col_b.at[:, sub_of(p)], col_b_in.at[s], B_COL)
    push_all(TW, tgt_peer, lambda p: row_b, row_b_in.at[t], B_ROW)
    col_b_in[s] = col_b[:, my_sub]
    row_b_in[t] = row_b[...]
    wait_in(xg.at[pl.ds(0, 2), 0], G_RING3)
    before, after = lax.rem(z + ZS - 3, ZS), lax.rem(z + 3, ZS)
    top, rest = pl.ds(0, 16), pl.ds(16, 16)
    push(xg.at[before, core, top], xg.at[before, core, top], G_RING4, z_peer(1))
    push(xg.at[after, core, rest], xg.at[after, core, rest], G_RING4, z_peer(ZS - 1))
    vec_t[2:3, :] = res1[2]
    vec_s[:, 1, :] = res0[1]
    vec_s[:, 2, :] = res1[1]
    row_sums(2, 3)
    col_sums(0, 3, 0, 3)
    col_sums(0, 3, 6, 8)

    wait_in(row_b_in.at[pl.ds(0, TW - 1)], B_ROW)
    row_full1 = jnp.sum(row_b_in[...], axis=0)
    agz_b[z] = row_full1
    wait_in(col_b_in.at[pl.ds(0, SW - 1)], B_COL)
    col_full1 = jnp.sum(col_b_in[...], axis=0)
    agc_b[:, my_sub] = col_full1[0:1, :]
    sc2_out[0] = col_full1[1:2, :]

    push_all(SW, src_peer, lambda p: agc_b.at[:, my_sub], agc_b.at[:, my_sub], B_AGC)
    push_all(TW, tgt_peer, lambda p: sc2_out.at[0], ags_b_in.at[t], B_AGS)
    push_all(ZS, z_peer, lambda p: agz_b.at[z], agz_b.at[z], B_AGZ)
    ags_b_in[t] = sc2_out[0]
    wait_in(xg.at[0, 0], G_RING4)
    for p in (3, ZS - 3, 4):
        zz = lax.rem(z + p, ZS)
        push(xg.at[zz, core], xg.at[zz, core], G_SIB2, sibling)
    wait_in(xg.at[pl.ds(0, 3), 0], G_SIB2)
    lax.fori_loop(3, 6, q_block, 0)
    col_sums(0, 3, 3, 6)

    wait_in(agz_b.at[pl.ds(0, ZS - 1)], B_AGZ)
    wait_in(ags_b_in.at[pl.ds(0, TW - 1)], B_AGS)
    wait_in(agc_b.at[:, pl.ds(0, (SW - 1) * SUB)], B_AGC)
    sums = jnp.sum(ags_b_in[...], axis=0)
    norm1 = lane(sums, 0)
    beta0 = norm1 / norm0
    alpha1 = norm1 / (lane(sums, 1) - beta0 * norm1 / alpha0)
    prod1 = [row_full1, agz_b[:, 0, :], agc_b[...]]
    dir1 = [r1 + beta0 * r0 for r1, r0 in zip(res1, res0)]
    image1 = [d * r + v + beta0 * i for d, r, v, i in zip(diag, res1, prod1, image0)]
    res2 = [r - alpha1 * i for r, i in zip(res1, image1)]
    sol2 = [alpha0 * r0 + alpha1 * d1 for r0, d1 in zip(res0, dir1)]

    row_part = matvec(res2[0], res2[2], False)
    sc_out[...] = scalars(res2, row_part)

    push_all(SW, src_peer, lambda p: sc_out, sc_in.at[s], C_SRC)
    sc_in[s] = sc_out[...]

    vec_t[3:4, :] = res2[2]
    vec_s[:, 3, :] = res2[1]
    first_step = alpha0 + alpha1 * beta0

    def sums_of(points, out, v):
        low = v * STACK
        return points * out[low + 64:low + 65, :] - out[low:low + 64, :]

    def early_gradients(points, out, own, write):
        ones = sums_of(points, out, 0)
        zeroth = sums_of(points, out, 1)
        latest = sums_of(points, out, 2)
        write(0, (1.0 + first_step * own[0] + alpha1 * own[1]) * ones + first_step * zeroth + alpha1 * latest)
        write(1, (own[1] + beta0 * own[0]) * ones + latest + beta0 * zeroth)

    def late_gradient(points, out, own, write):
        write(2, own[2] * sums_of(points, out, 0) + sums_of(points, out, 3))

    def write_col(part, value):
        for k in range(XS):
            g_col[part, k] = value[k * 16:(k + 1) * 16, :]

    def write_row(part, value):
        for k in range(TW):
            g_row[part, k] = value[k * 8:(k + 1) * 8, :]

    early, late = pl.ds(0, 2), pl.ds(2, 1)
    own_t = vec_t[:, my_tile]
    own_t = [own_t[v:v + 1, :] for v in range(1, VECS)]
    own_s = [res0[0], res1[0], res2[0]]
    early_gradients(ysub[...], t_col, own_t, write_col)
    push_all(XS, x_peer, lambda p: g_col.at[early, lax.rem(x + p, XS)], g_col_in.at[x, early], D_COL)
    early_gradients(xs, t_row, own_s, write_row)
    push_all(TW, tgt_peer, lambda p: g_row.at[early, lax.rem(t + p, TW)], g_row_in.at[t, early], D_ROW)
    col_sums(3, 4)
    late_gradient(ysub[...], t_col, own_t, write_col)
    push_all(XS, x_peer, lambda p: g_col.at[late, lax.rem(x + p, XS)], g_col_in.at[x, late], D_COL2)
    g_col_in[x] = g_col[:, x]
    wait_in(sc_in.at[pl.ds(0, SW - 1)], C_SRC)
    sc2_out[1] = jnp.sum(sc_in[...], axis=0)
    push_all(TW, tgt_peer, lambda p: sc2_out.at[1], sc2_in.at[t], C_TGT)
    sc2_in[t] = sc2_out[1]

    row_sums(3, 4)
    late_gradient(xs, t_row, own_s, write_row)
    push_all(TW, tgt_peer, lambda p: g_row.at[late, lax.rem(t + p, TW)], g_row_in.at[t, late], D_ROW2)
    g_row_in[t] = g_row[:, t]

    wait_in(sc2_in.at[pl.ds(0, TW - 1)], C_TGT)
    sums = jnp.sum(sc2_in[...], axis=0)
    norm2 = lane(sums, 0)
    beta1 = norm2 / norm1
    alpha2 = norm2 / (lane(sums, 1) - beta1 * norm2 / alpha1)
    both = alpha2 * beta1

    def combine(parts):
        return (parts[0] + both * parts[1] + alpha2 * parts[2]) * (1.0 / EPSILON)

    def lead_of(zz):
        return pl.ds(pl.multiple_of(zz * TILE, TILE), LEAD)

    def rest_of(zz):
        return pl.ds(pl.multiple_of(zz * TILE + LEAD, 128), TILE - LEAD)

    wait_in(g_col_in.at[pl.ds(0, XS - 1), early], D_COL)
    wait_in(g_col_in.at[pl.ds(0, XS - 1), late], D_COL2)
    gt_ref[x, :, my_tile] = combine(jnp.sum(g_col_in[...], axis=0))
    mine = gt_ref.at[x, :, rest_of(z)]
    push_all(XS, x_peer, lambda p: mine, mine, O_XX)
    for p in (1, ZS - 1, 2, ZS - 2, 3, ZS - 3, 4):
        push(gt_ref.at[x, :, lead_of(z)], gt_ref.at[x, :, lead_of(z)], O_ZF, z_peer(p), IN_ZF + p)

    def lead_along_x(zz):
        for p in range(1, XS):
            push(gt_ref.at[x, :, lead_of(zz)], gt_ref.at[x, :, lead_of(zz)], O_ZF, x_peer(p), IN_XF + p)

    lead_along_x(z)

    sol_src_ref[...] = sol2[0] + both * dir1[0] + alpha2 * res2[0]
    sol_tgt_ref[...] = sol2[2] + both * dir1[2] + alpha2 * res2[2]

    wait_in(gt_ref.at[pl.ds(0, XS - 1), :, pl.ds(0, TILE - LEAD)], O_XX)
    push_all(
        ZS, z_peer, lambda p: gt_ref.at[:, :, rest_of(z)], gt_ref.at[:, :, rest_of(z)], O_XZ
    )
    for p in (1, ZS - 1, 2, ZS - 2, 3, ZS - 3, 4):
        zz = lax.rem(z + ZS - p, ZS)
        wait_in(gt_ref.at[x, :, lead_of(zz)], IN_ZF + p)
        lead_along_x(zz)
        if p == ZS - 1:
            wait_in(g_row_in.at[pl.ds(0, TW - 1), early], D_ROW)
            wait_in(g_row_in.at[pl.ds(0, TW - 1), late], D_ROW2)
            gs_ref[t] = combine(jnp.sum(g_row_in[...], axis=0))
            push_all(TW, tgt_peer, lambda p: gs_ref.at[t], gs_ref.at[t], O_ROW)

    wait_in(gs_ref.at[pl.ds(0, TW - 1)], O_ROW)
    wait_in(gt_ref.at[:, :, pl.ds(0, (ZS - 1) * (TILE - LEAD))], O_XZ)
    for p in range(1, XS):
        wait_in(gt_ref.at[0, :, pl.ds(0, ZS * LEAD)], IN_XF + p)

    wait_out(col_a_in.at[pl.ds(0, SW - 1)], A_COL)
    wait_out(row_a_in.at[pl.ds(0, TW - 1)], A_ROW)
    wait_out(init_in.at[pl.ds(0, ZS - 1)], A_INIT)
    wait_out(agc_a.at[:, pl.ds(0, (SW - 1) * SUB)], A_AGC)
    wait_out(agz_a.at[pl.ds(0, ZS - 1)], A_AGZ)
    wait_out(ags_a_in.at[pl.ds(0, TW - 1)], A_AGS)
    wait_out(col_b_in.at[pl.ds(0, SW - 1)], B_COL)
    wait_out(row_b_in.at[pl.ds(0, TW - 1)], B_ROW)
    wait_out(agc_b.at[:, pl.ds(0, (SW - 1) * SUB)], B_AGC)
    wait_out(agz_b.at[pl.ds(0, ZS - 1)], B_AGZ)
    wait_out(ags_b_in.at[pl.ds(0, TW - 1)], B_AGS)
    wait_out(sc_in.at[pl.ds(0, SW - 1)], C_SRC)
    wait_out(sc2_in.at[pl.ds(0, TW - 1)], C_TGT)
    wait_out(g_row_in.at[pl.ds(0, TW - 1), early], D_ROW)
    wait_out(g_col_in.at[pl.ds(0, XS - 1), early], D_COL)
    wait_out(g_row_in.at[pl.ds(0, TW - 1), late], D_ROW2)
    wait_out(g_col_in.at[pl.ds(0, XS - 1), late], D_COL2)
    wait_out(gs_ref.at[pl.ds(0, TW - 1)], O_ROW)
    wait_out(gt_ref.at[pl.ds(0, XS - 1), :, pl.ds(0, TILE - LEAD)], O_XX)
    wait_out(gt_ref.at[:, :, pl.ds(0, (ZS - 1) * (TILE - LEAD))], O_XZ)
    wait_out(gt_ref.at[pl.ds(0, 3), :, pl.ds(0, ZS * LEAD)], O_ZF)
    wait_out(gt_ref.at[0, :, pl.ds(0, (ZS - 1) * LEAD)], O_ZF)
    for k in (G_RING1, G_RING2, G_RING3):
        wait_out(xg.at[pl.ds(0, 2), 0], k)
    wait_out(xg.at[0, 0], G_RING4)
    wait_out(xg.at[pl.ds(0, 4), 0], G_SIB1)
    wait_out(xg.at[pl.ds(0, 3), 0], G_SIB2)


def hand_out(*refs):
    sems = refs[-1]
    parts = [(refs[3].at[k], refs[7].at[k], refs[11].at[k]) for k in range(XS)]
    parts += [(refs[k], refs[4 + k], refs[8 + k]) for k in (2, 1, 0)]
    loads = [pltpu.make_async_copy(src, near, sems.at[k]) for k, (src, _, near) in enumerate(parts)]
    stores = [
        pltpu.make_async_copy(near, dst, sems.at[len(parts) + k])
        for k, (_, dst, near) in enumerate(parts)
    ]
    for load in loads:
        load.start()
    for load, store in zip(loads, stores):
        load.wait()
        store.start()
    for store in stores:
        store.wait()


def body(src_points, tgt_points, src_potential, tgt_potential, src_rhs, tgt_rhs):
    normalizer = 1.0 / math.sqrt(NS * SW * NT * TW)
    vmem = pl.BlockSpec(memory_space=pltpu.VMEM)
    far = pl.BlockSpec(memory_space=pltpu.HBM)

    def buf(*shape, dtype=F32):
        return pltpu.VMEM(shape, dtype)

    scratch = [
        buf(2, DIM // 2, NS), buf(DIM, NT), buf(1, NS), buf(1, NT), buf(1, NS), buf(1, NT),
        pltpu.SemaphoreType.DMA((6,)),
        buf(NS, NT), buf(NS, NT, dtype=BF16), buf(NS, NT, dtype=BF16),
        buf(ZS, NS, TILE, dtype=BF16), buf(ZS, NS, TILE, dtype=BF16),
        buf(NS, 256, dtype=BF16), buf(256, NT, dtype=BF16),
        buf(NS, 128), buf(NS, 128), buf(NS, 128), buf(NS, 128),
        buf(4, NT), buf(SW, 4, SUB), buf(2, NS), buf(TW, 2, NS),
        buf(2, NS), buf(ZS, 2, NS),
        buf(2, NT), buf(ZS, 2, NS), buf(1, 128), buf(TW, 1, 128),
        buf(2, NT), buf(SW, 2, SUB), buf(1, NS), buf(TW, 1, NS),
        buf(1, NT), buf(ZS, 1, NS), buf(TW, 1, 128),
        buf(1, 128), buf(SW, 1, 128), buf(2, 1, 128), buf(TW, 1, 128),
        buf(DIM, TILE), buf(VECS, NT), buf(ZS, VECS, NS),
        buf(2 * 3 * STACK, TILE, dtype=BF16),
        buf(VECS * STACK, NS), buf(VECS * STACK, TILE),
        buf(3, TW, 8, NS), buf(TW, 3, 8, NS),
        buf(3, XS, 16, TILE), buf(XS, 3, 16, TILE),
        buf(ZS, 2, DIM // 2, NS),
        pltpu.SemaphoreType.DMA((N_SEMS,)), pltpu.SemaphoreType.DMA((N_IN,)),
    ]
    shapes = (
        jax.ShapeDtypeStruct((1, NS), F32),
        jax.ShapeDtypeStruct((1, NT), F32),
        jax.ShapeDtypeStruct((TW, 8, NS), F32),
        jax.ShapeDtypeStruct((XS, 16, NT), F32),
    )
    results = pl.pallas_call(
        functools.partial(kernel, math.log2(normalizer)),
        out_shape=shapes,
        in_specs=[far] * 6,
        out_specs=[vmem] * 4,
        scratch_shapes=scratch,
        compiler_params=pltpu.CompilerParams(
            collective_id=1, has_side_effects=True, vmem_limit_bytes=60 * 1024 * 1024
        ),
    )(
        src_points.reshape(2, DIM // 2, NS), tgt_points, src_potential.reshape(1, NS),
        tgt_potential.reshape(1, NT), src_rhs.reshape(1, NS), tgt_rhs.reshape(1, NT),
    )
    sol_src, sol_tgt, grad_src, grad_tgt = pl.pallas_call(
        hand_out,
        out_shape=shapes,
        in_specs=[far] * 4,
        out_specs=[far] * 4,
        scratch_shapes=[buf(*shape.shape) for shape in shapes] + [pltpu.SemaphoreType.DMA((2 * (XS + 3),))],
        compiler_params=pltpu.CompilerParams(vmem_limit_bytes=60 * 1024 * 1024),
    )(*results)
    return (
        sol_src.reshape(NS), sol_tgt.reshape(NT), grad_src.reshape(DIM, NS), grad_tgt.reshape(DIM, NT)
    )


def solution(mesh):
    return jax.shard_map(
        body,
        mesh=mesh,
        in_specs=(P(None, "src"), P(None, "tgt"), P("src"), P("tgt"), P("src"), P("tgt")),
        out_specs=(P("src"), P("tgt"), P(None, "src"), P(None, "tgt")),
        check_vma=False,
    )
```
